256 devices in a mesh: segment: 4 (over x), dom: 32 (over z, y), dp: 2 (over core).
Axes of the slice: x: 4, y: 4, z: 8, core: 2. Of those that a mesh axis runs over, the one named last changes fastest.
Arguments:
- node_in: bfloat16 [4, 4096, 512], P('dp', 'dom'), may hold values from -6 to 6
- edge_in: bfloat16 [4, 4096, 512], P('dp', 'dom'), may hold values from -6 to 6
- node_cot: bfloat16 [4, 4096, 512], P('dp', 'dom'), may hold values from -6 to 6
- edge_cot: bfloat16 [4, 4096, 512], P('dp', 'dom'), may hold values from -6 to 6
- send_rows: int32 [4096], P('dom'), may hold values from 0 to 127
- sender_row: int32 [4096], P('dom'), may hold values from 0 to 255
- receiver_row: int32 [4096], P('dom'), may hold values from 0 to 127
- edge_count: int32 [32], P('dom'), may hold values from 1 to 128, 3072 in all
- edge_w1: bfloat16 [4, 1536, 512], P('segment'), may hold values from -0.15625 to 0.15625
- edge_w2: bfloat16 [4, 512, 512], P('segment'), may hold values from -0.25 to 0.25
- node_w1: bfloat16 [4, 1024, 512], P('segment'), may hold values from -0.1875 to 0.1875
- node_w2: bfloat16 [4, 512, 512], P('segment'), may hold values from -0.25 to 0.25
- vectors: bfloat16 [4, 8, 512], P('segment'), may hold values from -2 to 2, as said below
Outputs:
- node_out: bfloat16 [4, 4, 4096, 512], P('segment', 'dp', 'dom')
- edge_out: bfloat16 [4, 4, 4096, 512], P('segment', 'dp', 'dom')
- node_grad: float32 [4, 4, 4096, 512], P('segment', 'dp', 'dom')
- edge_grad: float32 [4, 4, 4096, 512], P('segment', 'dp', 'dom')
- grad_edge_w1: float32 [4, 1536, 512], P('segment', None, ('dom', 'dp'))
- grad_edge_w2: float32 [4, 512, 512], P('segment', None, ('dom', 'dp'))
- grad_node_w1: float32 [4, 1024, 512], P('segment', None, ('dom', 'dp'))
- grad_node_w2: float32 [4, 512, 512], P('segment', None, ('dom', 'dp'))
- grad_vectors: float32 [4, 8, 512], P('segment', None, ('dom', 'dp'))
The draws below stay inside these ranges and needn't reach their ends.
Inputs may be any that keep to these rules, and one draw needn't show every extreme that they name: `vectors`: the parameter rows 2 and 6 of each layer are norm gains between 0.5 and 1.5, the others offsets. `edge_count`: one partition has all 128 slots live.
All inputs are finite; a program needn't handle non-finite values. No bound on the sum of `edge_count` on one device may be relied on, other than what follows from the above.
Results may differ from the reference program's by a relative error of at most 0.02.
Values may be sent and summed in bfloat16 or wider, within the bound.
A program may use at most 128 MiB of HBM per device.

```python
import math
import jax
import jax.numpy as jnp
import numpy as np
from jax import lax

D = 512
NODE_DEV = 128
HALO = 64
EDGE_DEV = 128
LAYERS = 4
PARTITIONS = 32
NODES = 4096
EDGES = 4096
SAMPLES = 4
SENDS = 4096


def draw_vectors(key, part):
    normal_key, uniform_key = jax.random.split(key)
    offsets = jnp.clip(0.5 * jax.random.normal(normal_key, (LAYERS, 8, D), jnp.float32), -2.0, 2.0)
    gains = jax.random.uniform(uniform_key, (LAYERS, 8, D), jnp.float32, 0.5, 1.5)
    row_ids = jnp.arange(8, dtype=jnp.int32)
    gain_rows = ((row_ids == 2) | (row_ids == 6))[None, :, None]
    return jnp.where(gain_rows, gains, offsets).astype(jnp.bfloat16)


def with_ends(drawn, own_key, least, largest):
    dims = drawn.shape
    index_at = [jax.random.randint(jax.random.fold_in(own_key, axis), (), 0, dims[axis]) for axis in range(len(dims))]
    drawn = drawn.at[tuple(index_at)].set(least)
    longest = dims.index(max(dims))
    index_at[longest] = (index_at[longest] + 1) % dims[longest]
    return drawn.at[tuple(index_at)].set(largest)


def raised(entries, own_key, source, target, blocks, factor):
    owner, partner = [(jnp.arange(entries.shape[axis_at]) // (entries.shape[axis_at] // blocks)).reshape([-1 if axis == axis_at else 1 for axis in range(entries.ndim)]) for axis_at in (source, target)]
    chosen = jax.random.permutation(own_key, blocks)[partner]
    strong = (owner == chosen) | (owner == (partner + blocks // 2) % blocks)
    return jnp.where(strong, factor * entries, entries)


def levels(own_key, extent, cuts, smallest, high):
    def one(axis_at, parts):
        heights = jax.random.uniform(jax.random.fold_in(jax.random.fold_in(own_key, 6), axis_at), (parts,), jnp.float32, smallest / len(cuts), high / len(cuts))
        return jnp.repeat(jnp.exp(heights), extent[axis_at] // parts).reshape((-1,) + (1,) * (len(extent) - axis_at - 1))

    loudness = one(*cuts[0])
    for cut in cuts[1:]:
        loudness = loudness * one(*cut)
    return loudness


def split_up(amount, total, limit, lean):
    loads = [(1 << 20) // math.isqrt(standing ** lean) + 1 for standing in range(2, amount + 1)]
    rest, holding = total - limit - (amount - 1), [1] * (amount - 1)
    while rest > 0:
        movable = [i for i in range(amount - 1) if holding[i] < limit]
        pool, budget = sum([loads[i] for i in movable]), rest
        for i in movable:
            extra = min(limit - holding[i], max(1, budget * loads[i] // pool), rest)
            holding[i] = holding[i] + extra
            rest = rest - extra
    return np.array([limit] + holding)


def uneven_parts(rng, amount, total, limit, lean):
    if amount == 2:
        one = jax.random.randint(rng, (), max(1, total - limit), min(limit, total - 1) + 1)
        return jnp.stack([one, total - one])
    sizes = jnp.asarray(split_up(amount, total, limit, lean), jnp.int32)
    twos = (amount - 1) // 2
    giver, receiver = sizes[1:1 + 2 * twos:2], sizes[2:2 + 2 * twos:2]
    room = jnp.minimum(giver - 1, limit - receiver)
    moved = jax.random.randint(jax.random.fold_in(rng, 1), (twos,), 0, 1 << 20) % (room + 1)
    sizes = sizes.at[1:1 + 2 * twos:2].set(giver - moved).at[2:2 + 2 * twos:2].set(receiver + moved)
    return sizes[jax.random.permutation(jax.random.fold_in(rng, 2), amount)]


def bell_draw(stream_key, dims, width, reach, cuts=(), kind=jnp.bfloat16):
    result = width * jax.random.normal(stream_key, dims, jnp.float32)
    if cuts:
        result = result * levels(stream_key, dims, cuts, -0.22, 0.18)
    return jnp.clip(result, -reach, reach).astype(kind)


def bell_draw_with(key, extent, deviation, most, cuts, heavy, kind=jnp.bfloat16):
    drawn = deviation * jax.random.normal(key, extent, jnp.float32)
    if cuts:
        drawn = drawn * levels(key, extent, cuts, -0.22, 0.18)
    return jnp.clip(raised(drawn, jax.random.fold_in(key, 3), *heavy), -most, most).astype(kind)


def setup_inputs(seed: int = 0) -> dict:
    key_of = jax.random.split(jax.random.key(seed), 14)
    return {
        "node_in": bell_draw(key_of[0], (SAMPLES, NODES, D), 1.0, 6.0, ((0, 2), (1, 32))),
        "edge_in": bell_draw(key_of[1], (SAMPLES, EDGES, D), 1.0, 6.0, ((0, 2), (1, 32))),
        "node_cot": bell_draw_with(key_of[2], (SAMPLES, NODES, D), 1.0, 6.0, ((0, 2), (1, 32)), (1, 2, 32, 2.75)),
        "edge_cot": bell_draw(key_of[3], (SAMPLES, EDGES, D), 1.0, 6.0, ((0, 2), (1, 32))),
        "send_rows": with_ends(jax.random.randint(key_of[4], (SENDS,), 0, NODE_DEV), jax.random.fold_in(key_of[4], 1), 0, NODE_DEV - 1).astype(jnp.int32),
        "sender_row": with_ends(jax.random.randint(key_of[5], (EDGES,), 0, NODE_DEV + 2 * HALO), jax.random.fold_in(key_of[5], 1), 0, (NODE_DEV + 2 * HALO) - 1).astype(jnp.int32),
        "receiver_row": with_ends(jax.random.randint(key_of[6], (EDGES,), 0, NODE_DEV), jax.random.fold_in(key_of[6], 1), 0, NODE_DEV - 1).astype(jnp.int32),
        "edge_count": uneven_parts(key_of[7], PARTITIONS, PARTITIONS * EDGE_DEV * 3 // 4, EDGE_DEV, 2).astype(jnp.int32),
        "edge_w1": bell_draw(key_of[8], (LAYERS, 3 * D, D), (3 * D) ** -0.5, 0.15625, ((0, 4),)),
        "edge_w2": bell_draw(key_of[9], (LAYERS, D, D), D ** -0.5, 0.25, ((0, 4),)),
        "node_w1": bell_draw(key_of[10], (LAYERS, 2 * D, D), (2 * D) ** -0.5, 0.1875, ((0, 4),)),
        "node_w2": bell_draw(key_of[11], (LAYERS, D, D), D ** -0.5, 0.25, ((0, 4),)),
        "vectors": draw_vectors(jax.random.fold_in(key_of[13], 71), 0),
    }


def layer_norm(values):
    average = lax.optimization_barrier(jnp.mean(values, -1, keepdims=True))
    centred = values - average
    return centred * lax.rsqrt(lax.optimization_barrier(jnp.mean(centred * centred, -1, keepdims=True)) + 1e-05)

def layer_local(node_rows, halo_rows, edge_rows, probes, weights, graph_lists):
    edge_w1, edge_w2, node_w1, node_w2, vectors = weights
    sender_row, receiver_row, live_mask = graph_lists
    coeffs = vectors.astype(jnp.float32)
    node_half = node_rows.astype(jnp.bfloat16)
    node_table = jnp.concatenate([node_half, halo_rows.astype(jnp.bfloat16)], 0)
    pick_send = (sender_row[:, None] == jnp.arange(node_table.shape[0], dtype=jnp.int32)[None, :]).astype(jnp.bfloat16)
    pick_recv = (receiver_row[:, None] == jnp.arange(node_rows.shape[0], dtype=jnp.int32)[None, :]).astype(jnp.bfloat16)
    senders = jnp.dot(pick_send, node_table, preferred_element_type=jnp.float32).astype(jnp.bfloat16)
    receivers = jnp.dot(pick_recv, node_half, preferred_element_type=jnp.float32).astype(jnp.bfloat16)
    joined = jnp.concatenate([edge_rows.astype(jnp.bfloat16), senders, receivers], 1)
    edge_pre = jnp.dot(joined, edge_w1, preferred_element_type=jnp.float32) + coeffs[0] + probes[0]
    edge_hid = jax.nn.silu(edge_pre).astype(jnp.bfloat16)
    edge_lin = jnp.dot(edge_hid, edge_w2, preferred_element_type=jnp.float32) + coeffs[1] + probes[1]
    edge_norm = layer_norm(edge_lin)
    message = (edge_norm * coeffs[2] + coeffs[3] + probes[2]) * live_mask[:, None]
    edge_next = edge_rows + message
    incoming = lax.dot_general(pick_recv, message.astype(jnp.bfloat16), (((0,), (0,)), ((), ())), preferred_element_type=jnp.float32)
    node_cat = jnp.concatenate([node_half, incoming.astype(jnp.bfloat16)], 1)
    node_pre = jnp.dot(node_cat, node_w1, preferred_element_type=jnp.float32) + coeffs[4] + probes[3]
    node_hid = jax.nn.silu(node_pre).astype(jnp.bfloat16)
    node_lin = jnp.dot(node_hid, node_w2, preferred_element_type=jnp.float32) + coeffs[5] + probes[4]
    node_norm = layer_norm(node_lin)
    node_next = node_rows + node_norm * coeffs[6] + coeffs[7] + probes[5]
    return ((node_next, edge_next), (joined, edge_hid, edge_norm, node_cat, node_hid, node_norm))

def blank_probes(node_count, edge_total, features):
    edge_zero = jnp.zeros((edge_total, features), jnp.float32)
    node_zero = jnp.zeros((node_count, features), jnp.float32)
    return (edge_zero, edge_zero, edge_zero, node_zero, node_zero, node_zero)

def transposed(left, cotangent):
    return lax.dot_general(left, cotangent.astype(jnp.bfloat16), (((0,), (0,)), ((), ())), preferred_element_type=jnp.float32)

def weight_grads(saved, probe_back):
    joined, edge_hid, edge_norm, node_cat, node_hid, node_norm = saved
    edge_pre_back, edge_lin_back, message_back, node_pre_back, node_lin_back, node_out_back = probe_back
    vector_back = jnp.stack([edge_pre_back.sum(0), edge_lin_back.sum(0), (message_back * edge_norm).sum(0), message_back.sum(0), node_pre_back.sum(0), node_lin_back.sum(0), (node_out_back * node_norm).sum(0), node_out_back.sum(0)], 0)
    return (transposed(joined, edge_pre_back), transposed(edge_hid, edge_lin_back), transposed(node_cat, node_pre_back), transposed(node_hid, node_lin_back), vector_back)

def forward_one(node_half, halo_half, edge_half, graph_lists, weights):
    probes = blank_probes(node_half.shape[0], edge_half.shape[0], node_half.shape[1])
    results, saved = layer_local(node_half.astype(jnp.float32), halo_half.astype(jnp.float32), edge_half.astype(jnp.float32), probes, weights, graph_lists)
    return (results[0].astype(jnp.bfloat16), results[1].astype(jnp.bfloat16))

def backward_one(node_half, halo_half, edge_half, node_back, edge_back, graph_lists, weights):
    probes = blank_probes(node_half.shape[0], edge_half.shape[0], node_half.shape[1])

    def local_layer(node_rows, halo_rows, edge_rows, probe_rows):
        return layer_local(node_rows, halo_rows, edge_rows, probe_rows, weights, graph_lists)
    results, pullback, saved = jax.vjp(local_layer, node_half.astype(jnp.float32), halo_half.astype(jnp.float32), edge_half.astype(jnp.float32), probes, has_aux=True)
    node_grad_in, halo_grad, edge_grad_in, probe_back = pullback((node_back, edge_back))
    return (node_grad_in, halo_grad, edge_grad_in, weight_grads(saved, probe_back))

def halo_of(node_half, send_lists):
    outgoing = jax.vmap(jnp.take, in_axes=(0, 0, None))(node_half, send_lists, 0)
    return jnp.concatenate([jnp.roll(outgoing, 1, 0)[:, HALO:], jnp.roll(outgoing, -1, 0)[:, :HALO]], 1)

def returned_of(halo_back):
    return jnp.concatenate([jnp.roll(halo_back, 1, 0)[:, HALO:], jnp.roll(halo_back, -1, 0)[:, :HALO]], 1)

def scatter_rows(values, row_ids):
    return jnp.zeros((NODE_DEV, values.shape[1]), jnp.float32).at[row_ids].add(values)

def reference(node_in, edge_in, node_cot, edge_cot, send_rows, sender_row, receiver_row, edge_count, edge_w1, edge_w2, node_w1, node_w2, vectors):
    partitions = PARTITIONS
    send_lists = send_rows.reshape(partitions, 2 * HALO)
    live_mask = (jnp.arange(EDGE_DEV, dtype=jnp.int32)[None, :] < edge_count[:, None]).astype(jnp.float32)
    graph_lists = (sender_row.reshape(partitions, EDGE_DEV), receiver_row.reshape(partitions, EDGE_DEV), live_mask)
    forward_map = jax.vmap(forward_one, in_axes=(0, 0, 0, 0, None))
    backward_map = jax.vmap(backward_one, in_axes=(0, 0, 0, 0, 0, 0, None))
    node_outs = [[] for layer_index in range(LAYERS)]
    edge_outs = [[] for layer_index in range(LAYERS)]
    node_grads = [[] for layer_index in range(LAYERS)]
    edge_grads = [[] for layer_index in range(LAYERS)]
    grad_store = [None for layer_index in range(LAYERS)]
    for sample in range(SAMPLES):
        node_half = node_in[sample].reshape(partitions, NODE_DEV, D)
        edge_half = edge_in[sample].reshape(partitions, EDGE_DEV, D)
        stored = []
        for layer_index in range(LAYERS):
            weights = (edge_w1[layer_index], edge_w2[layer_index], node_w1[layer_index], node_w2[layer_index], vectors[layer_index])
            halo_half = halo_of(node_half, send_lists)
            stored.append((node_half, halo_half, edge_half))
            node_half, edge_half = forward_map(node_half, halo_half, edge_half, graph_lists, weights)
            node_outs[layer_index].append(node_half.reshape(NODES, D))
            edge_outs[layer_index].append(edge_half.reshape(EDGES, D))
        node_back = node_cot[sample].astype(jnp.float32).reshape(partitions, NODE_DEV, D)
        edge_back = edge_cot[sample].astype(jnp.float32).reshape(partitions, EDGE_DEV, D)
        for layer_index in reversed(range(LAYERS)):
            weights = (edge_w1[layer_index], edge_w2[layer_index], node_w1[layer_index], node_w2[layer_index], vectors[layer_index])
            node_saved, halo_saved, edge_saved = stored[layer_index]
            node_back, halo_back, edge_back, grads = backward_map(node_saved, halo_saved, edge_saved, node_back, edge_back, graph_lists, weights)
            node_back = node_back + jax.vmap(scatter_rows)(returned_of(halo_back), send_lists)
            node_grads[layer_index].append(node_back.reshape(NODES, D))
            edge_grads[layer_index].append(edge_back.reshape(EDGES, D))
            summed = tuple((lax.optimization_barrier(jnp.sum(value, 0)) for value in grads))
            if grad_store[layer_index] is None:
                grad_store[layer_index] = summed
            else:
                grad_store[layer_index] = tuple((first + second for first, second in zip(grad_store[layer_index], summed)))
    node_out = jnp.stack([jnp.stack(node_outs[layer_index]) for layer_index in range(LAYERS)])
    edge_out = jnp.stack([jnp.stack(edge_outs[layer_index]) for layer_index in range(LAYERS)])
    node_grad = jnp.stack([jnp.stack(node_grads[layer_index]) for layer_index in range(LAYERS)])
    edge_grad = jnp.stack([jnp.stack(edge_grads[layer_index]) for layer_index in range(LAYERS)])
    grad_edge_w1 = jnp.stack([grad_store[layer_index][0] for layer_index in range(LAYERS)])
    grad_edge_w2 = jnp.stack([grad_store[layer_index][1] for layer_index in range(LAYERS)])
    grad_node_w1 = jnp.stack([grad_store[layer_index][2] for layer_index in range(LAYERS)])
    grad_node_w2 = jnp.stack([grad_store[layer_index][3] for layer_index in range(LAYERS)])
    grad_vectors = jnp.stack([grad_store[layer_index][4] for layer_index in range(LAYERS)])
    return (node_out, edge_out, node_grad, edge_grad, grad_edge_w1, grad_edge_w2, grad_node_w1, grad_node_w2, grad_vectors)
```

```python
import functools

import jax
import jax.numpy as jnp
from jax import lax
from jax.experimental import pallas as pl
from jax.experimental.pallas import tpu as pltpu
from jax.sharding import PartitionSpec as P

F32 = jnp.float32
BF16 = jnp.bfloat16
MESH = pl.DeviceIdType.MESH

D = 512
ROWS = 128
HALO = 64
SAMPLES = 2
NY = 4
NZ = 8
DOMS = NY * NZ
SECTIONS = 4
HALF = 1920
LANES_A = 1280
LANES_B = HALF - LANES_A


def dot_nn(left, right):
    return jnp.dot(left, right, preferred_element_type=F32)


def dot_nt(left, right):
    return lax.dot_general(left, right, (((1,), (1,)), ((), ())), preferred_element_type=F32)


def sigmoid(values):
    return 0.5 * jnp.tanh(0.5 * values) + 0.5


def norm_parts(values):
    average = jnp.mean(values, -1, keepdims=True)
    centred = values - average
    scale = lax.rsqrt(jnp.mean(centred * centred, -1, keepdims=True) + 1e-05)
    return centred * scale, scale


def norm_back(cotangent, normed, scale):
    first = jnp.mean(cotangent, -1, keepdims=True)
    second = jnp.mean(cotangent * normed, -1, keepdims=True)
    return scale * (cotangent - first - normed * second)


def column_sum(values):
    return jnp.sum(values, 0, keepdims=True)


def kernel(
    node_in,
    edge_in,
    node_cot,
    edge_cot,
    send_rows,
    sender_row,
    receiver_row,
    edge_count,
    w1e_hbm,
    w2e_hbm,
    w1n_hbm,
    w2n_hbm,
    vectors,
    node_out,
    edge_out,
    node_grad,
    edge_grad,
    grads_out,
    w1e,
    w2e,
    w1n,
    w2n,
    coeffs,
    table,
    edge_x,
    node_x,
    snd,
    rcv,
    hid_e,
    pre_e,
    norm_e,
    scale_e,
    inc,
    hid_n,
    pre_n,
    norm_n,
    scale_n,
    node_o,
    edge_o,
    send_buf,
    d_node,
    d_edge,
    d_node_f,
    d_edge_f,
    d_node_h,
    d_edge_h,
    halo_back,
    ret,
    cot_pe,
    cot_le,
    cot_pn,
    cot_ln,
    vec_acc,
    grad_half,
    grad_sib,
    sum_a,
    sum_b,
    recv_a1,
    recv_b1,
    half_a,
    half_b,
    recv_a2,
    recv_b2,
    fin,
    fin_sib,
    sem_local,
    sem_relay,
    sem_halo,
    sem_pair,
    sem_y,
    sem_z,
):
    seg = lax.axis_index("segment")
    dom = lax.axis_index("dom")
    core = lax.axis_index("dp")
    zed = dom // NY
    why = dom % NY
    first = seg == 0
    last = seg == SECTIONS - 1
    ahead = lax.rem(seg + 1, SECTIONS)
    behind = lax.rem(seg + SECTIONS - 1, SECTIONS)
    dom_next = lax.rem(dom + 1, DOMS)
    dom_prev = lax.rem(dom + DOMS - 1, DOMS)
    y_peers = [(seg, zed * NY + lax.rem(why + k, NY), core) for k in range(1, NY)]
    z_peers = [(seg, lax.rem(zed + k, NZ) * NY + why, core) for k in range(1, NZ)]
    sibling = (seg, dom, 1 - core)

    barrier = pltpu.get_barrier_semaphore()
    peers = y_peers + z_peers + [
        sibling,
        (ahead, dom, core),
        (behind, dom, core),
        (seg, dom_next, core),
        (seg, dom_prev, core),
    ]
    for peer in peers:
        pl.semaphore_signal(barrier, inc=1, device_id=peer, device_id_type=MESH)

    def local_copy(source, target, index):
        return pltpu.make_async_copy(source, target, sem_local.at[index])

    def span(sample):
        return pl.ds(sample * ROWS, ROWS)

    loads = [
        local_copy(w1e_hbm.at[0], w1e, 0),
        local_copy(w2e_hbm.at[0], w2e, 1),
        local_copy(w1n_hbm.at[0], w1n, 2),
        local_copy(w2n_hbm.at[0], w2n, 3),
    ]
    starts = []
    finals = []
    for sample in range(SAMPLES):
        starts.append(
            local_copy(node_in.at[sample], table.at[pl.ds(sample * 256, ROWS)], 4 + sample)
        )
        starts.append(local_copy(edge_in.at[sample], edge_x.at[span(sample)], 6 + sample))
        finals.append(local_copy(node_cot.at[sample], d_node.at[span(sample)], 8 + sample))
        finals.append(local_copy(edge_cot.at[sample], d_edge.at[span(sample)], 10 + sample))

    @pl.when(first)
    def _():
        for copy in starts:
            copy.start()

    for copy in loads:
        copy.start()

    @pl.when(last)
    def _():
        for copy in finals:
            copy.start()

    slots = lax.broadcasted_iota(jnp.int32, (2 * ROWS, ROWS), 0)
    own = slots[:ROWS]
    send_t = (own == send_rows[...]).astype(F32)
    recv_t = (own == receiver_row[...]).astype(F32)
    pick_t = (slots == sender_row[...]).astype(F32)
    send_pick = send_t.T.astype(BF16)
    recv_pick = recv_t.T.astype(BF16)
    sender_pick = pick_t.T.astype(BF16)
    send_t = send_t.astype(BF16)
    recv_t = recv_t.astype(BF16)
    pick_t = pick_t.astype(BF16)
    live = (lax.broadcasted_iota(jnp.int32, (ROWS, 1), 0) < edge_count[0]).astype(F32)
    coeffs[...] = vectors[...].astype(F32)

    def coeff(row):
        return coeffs[row : row + 1, :]

    def remote(source, target, sems, index, peer):
        return pltpu.make_async_remote_copy(
            src_ref=source,
            dst_ref=target,
            send_sem=sems.at[0, index],
            recv_sem=sems.at[1, index],
            device_id=peer,
            device_id_type=MESH,
        )

    def halo_copies(source, sample, target_ref, base, kind):
        return (
            remote(
                source.at[pl.ds(sample * ROWS, HALO)],
                target_ref.at[pl.ds(base + HALO, HALO)],
                sem_halo,
                kind * 4 + sample * 2,
                (seg, dom_prev, core),
            ),
            remote(
                source.at[pl.ds(sample * ROWS + HALO, HALO)],
                target_ref.at[pl.ds(base, HALO)],
                sem_halo,
                kind * 4 + sample * 2 + 1,
                (seg, dom_next, core),
            ),
        )

    def out_halo(sample):
        return halo_copies(send_buf, sample, table, sample * 256 + ROWS, 0)

    def back_halo(sample):
        return halo_copies(halo_back, sample, ret, sample * ROWS, 1)

    def node_relay(sample):
        return remote(
            node_o.at[span(sample)],
            table.at[pl.ds(sample * 256, ROWS)],
            sem_relay,
            sample,
            (ahead, dom, core),
        )

    def edge_relay(sample):
        return remote(
            edge_o.at[span(sample)],
            edge_x.at[span(sample)],
            sem_relay,
            2 + sample,
            (ahead, dom, core),
        )

    def node_return(sample):
        return remote(
            d_node_h.at[span(sample)],
            d_node.at[span(sample)],
            sem_relay,
            4 + sample,
            (behind, dom, core),
        )

    def edge_return(sample):
        return remote(
            d_edge_h.at[span(sample)],
            d_edge.at[span(sample)],
            sem_relay,
            6 + sample,
            (behind, dom, core),
        )

    def outputs(sample):
        return (
            local_copy(node_o.at[span(sample)], node_out.at[0, sample], 12 + sample),
            local_copy(edge_o.at[span(sample)], edge_out.at[0, sample], 14 + sample),
            local_copy(d_node_f.at[span(sample)], node_grad.at[0, sample], 16 + sample),
            local_copy(d_edge_f.at[span(sample)], edge_grad.at[0, sample], 18 + sample),
        )

    pl.semaphore_wait(barrier, len(peers))

    for sample in range(SAMPLES):
        rows = span(sample)
        own_rows = pl.ds(sample * 256, ROWS)

        @pl.when(first)
        def _():
            starts[2 * sample].wait()

        @pl.when(jnp.logical_not(first))
        def _():
            node_relay(sample).wait_recv()

        nodes = table[own_rows, :]
        node_x[rows, :] = nodes
        send_buf[rows, :] = dot_nn(send_pick, nodes).astype(BF16)
        for copy in out_halo(sample):
            copy.start()
        receivers = dot_nn(recv_pick, nodes).astype(BF16)
        rcv[rows, :] = receivers
        if sample == 0:
            for copy in loads:
                copy.wait()
        node_part = dot_nn(nodes, w1n[:D, :]) + coeff(4)
        edge_part = dot_nn(receivers, w1e[2 * D :, :]) + coeff(0)

        @pl.when(first)
        def _():
            starts[2 * sample + 1].wait()

        @pl.when(jnp.logical_not(first))
        def _():
            edge_relay(sample).wait_recv()

        edges = edge_x[rows, :]
        edge_part = edge_part + dot_nn(edges, w1e[:D, :])
        for copy in out_halo(sample):
            copy.wait_recv()
        senders = dot_nn(sender_pick, table[pl.ds(sample * 256, 256), :]).astype(BF16)
        snd[rows, :] = senders
        edge_pre = edge_part + dot_nn(senders, w1e[D : 2 * D, :])
        edge_hid = (edge_pre * sigmoid(edge_pre)).astype(BF16)
        pre_e[rows, :] = edge_pre
        hid_e[rows, :] = edge_hid
        edge_norm, edge_scale = norm_parts(dot_nn(edge_hid, w2e[...]) + coeff(1))
        norm_e[rows, :] = edge_norm
        scale_e[rows, :] = jnp.broadcast_to(edge_scale, (ROWS, 128))
        message = (edge_norm * coeff(2) + coeff(3)) * live
        edge_o[rows, :] = (edges.astype(F32) + message).astype(BF16)

        @pl.when(jnp.logical_not(last))
        def _():
            edge_relay(sample).start()

        incoming = dot_nn(recv_t, message.astype(BF16)).astype(BF16)
        inc[rows, :] = incoming
        node_pre = node_part + dot_nn(incoming, w1n[D:, :])
        node_hid = (node_pre * sigmoid(node_pre)).astype(BF16)
        pre_n[rows, :] = node_pre
        hid_n[rows, :] = node_hid
        node_norm, node_scale = norm_parts(dot_nn(node_hid, w2n[...]) + coeff(5))
        norm_n[rows, :] = node_norm
        scale_n[rows, :] = jnp.broadcast_to(node_scale, (ROWS, 128))
        node_o[rows, :] = (
            nodes.astype(F32) + node_norm * coeff(6) + coeff(7)
        ).astype(BF16)

        @pl.when(jnp.logical_not(last))
        def _():
            node_relay(sample).start()

        for copy in outputs(sample)[:2]:
            copy.start()

    def silu_slope(values):
        gate = sigmoid(values)
        return gate * (1.0 + values * (1.0 - gate))

    for sample in range(SAMPLES):
        rows = span(sample)

        @pl.when(last)
        def _():
            finals[2 * sample].wait()

        @pl.when(jnp.logical_not(last))
        def _():
            node_return(sample).wait_recv()

        node_back = d_node[rows, :].astype(F32)
        node_norm = norm_n[rows, :]
        node_lin_back = norm_back(node_back * coeff(6), node_norm, scale_n[rows, 0:1])
        lin_half = node_lin_back.astype(BF16)
        cot_ln[rows, :] = lin_half
        node_pre_back = dot_nt(lin_half, w2n[...]).astype(BF16).astype(F32) * silu_slope(
            pre_n[rows, :]
        )
        pre_half = node_pre_back.astype(BF16)
        cot_pn[rows, :] = pre_half
        node_total = node_back + dot_nt(pre_half, w1n[:D, :]).astype(BF16).astype(F32)
        incoming_back = dot_nt(pre_half, w1n[D:, :]).astype(BF16)

        @pl.when(last)
        def _():
            finals[2 * sample + 1].wait()

        @pl.when(jnp.logical_not(last))
        def _():
            edge_return(sample).wait_recv()

        edge_back = d_edge[rows, :].astype(F32)
        edge_norm = norm_e[rows, :]
        message_back = (edge_back + dot_nn(recv_pick, incoming_back)) * live
        edge_lin_back = norm_back(message_back * coeff(2), edge_norm, scale_e[rows, 0:1])
        lin_half = edge_lin_back.astype(BF16)
        cot_le[rows, :] = lin_half
        edge_pre_back = dot_nt(lin_half, w2e[...]).astype(BF16).astype(F32) * silu_slope(
            pre_e[rows, :]
        )
        pre_half = edge_pre_back.astype(BF16)
        cot_pe[rows, :] = pre_half
        sender_back = dot_nt(pre_half, w1e[D : 2 * D, :]).astype(BF16)
        halo_back[rows, :] = dot_nn(pick_t[ROWS:, :], sender_back).astype(BF16)
        for copy in back_halo(sample):
            copy.start()
        edge_total = edge_back + dot_nt(pre_half, w1e[:D, :]).astype(BF16).astype(F32)
        d_edge_f[rows, :] = edge_total
        d_edge_h[rows, :] = edge_total.astype(BF16)

        @pl.when(jnp.logical_not(first))
        def _():
            edge_return(sample).start()

        receiver_back = dot_nt(pre_half, w1e[2 * D :, :]).astype(BF16)
        node_total = node_total + dot_nn(pick_t[:ROWS, :], sender_back).astype(BF16).astype(F32)
        node_total = node_total + dot_nn(recv_t, receiver_back).astype(BF16).astype(F32)
        sums = (
            edge_pre_back,
            edge_lin_back,
            message_back * edge_norm,
            message_back,
            node_pre_back,
            node_lin_back,
            node_back * node_norm,
            node_back,
        )
        for index, value in enumerate(sums):
            vec_acc[sample, index : index + 1, :] = column_sum(value)
        for copy in back_halo(sample):
            copy.wait_recv()
        node_total = node_total + dot_nn(send_t, ret[rows, :])
        d_node_f[rows, :] = node_total
        d_node_h[rows, :] = node_total.astype(BF16)

        @pl.when(jnp.logical_not(first))
        def _():
            node_return(sample).start()

        for copy in outputs(sample)[2:]:
            copy.start()

    def put(start, value):
        width = value.shape[1]
        here = value.astype(BF16)
        if start >= HALF:
            grad_half[1, :, start - HALF : start - HALF + width] = here
        elif start + width <= HALF:
            grad_half[0, :, start : start + width] = here
        else:
            cut = HALF - start
            grad_half[0, :, start:HALF] = here[:, :cut]
            grad_half[1, :, 0 : width - cut] = here[:, cut:]

    edge_pre_t = cot_pe[...].T
    put(0, dot_nn(edge_pre_t, edge_x[...]))
    put(D, dot_nn(edge_pre_t, snd[...]))
    put(2 * D, dot_nn(edge_pre_t, rcv[...]))
    put(3 * D, dot_nn(cot_le[...].T, hid_e[...]))
    node_pre_t = cot_pn[...].T
    put(4 * D, dot_nn(node_pre_t, node_x[...]))
    put(5 * D, dot_nn(node_pre_t, inc[...]))
    put(6 * D, dot_nn(cot_ln[...].T, hid_n[...]))
    vec_sum = vec_acc[0] + vec_acc[1]
    vec_block = jnp.concatenate([vec_sum, jnp.zeros((120, D), F32)], 0).T
    put(7 * D, jnp.concatenate([vec_block, jnp.zeros((D, 128), F32)], 1))

    pair = remote(grad_half.at[1 - core], grad_sib, sem_pair, 0, sibling)
    pair.start()
    pair.wait()
    for z_at in range(NZ):
        here = pl.ds(z_at * NY * 16, NY * 16)
        total = grad_half[core, here, :].astype(F32) + grad_sib[here, :].astype(F32)
        total = total.astype(BF16).reshape(NY, 16, HALF)
        sum_a[z_at] = total[:, :, :LANES_A]
        sum_b[z_at] = total[:, :, LANES_A:]

    copies = []
    for k in range(1, NY):
        target = lax.rem(why + k, NY)
        copies.append(
            remote(sum_a.at[:, target], recv_a1.at[k - 1], sem_y, k - 1, y_peers[k - 1])
        )
    for k in range(1, NZ):
        target = lax.rem(zed + k, NZ)
        copies.append(
            remote(sum_b.at[target], recv_b1.at[k - 1], sem_z, k - 1, z_peers[k - 1])
        )
    for copy in copies:
        copy.start()
    for copy in copies[: NY - 1]:
        copy.wait_recv()
    for z_at in range(NZ):
        total = sum_a[z_at, why].astype(F32)
        for k in range(NY - 1):
            total = total + recv_a1[k, z_at].astype(F32)
        half_a[z_at] = total.astype(BF16)
    copies_2 = []
    for k in range(1, NZ):
        target = lax.rem(zed + k, NZ)
        copies_2.append(
            remote(half_a.at[target], recv_a2.at[k - 1], sem_z, NZ - 2 + k, z_peers[k - 1])
        )
    for copy in copies_2:
        copy.start()
    for copy in copies[NY - 1 :]:
        copy.wait_recv()
    for y_at in range(NY):
        total = sum_b[zed, y_at].astype(F32)
        for k in range(NZ - 1):
            total = total + recv_b1[k, y_at].astype(F32)
        half_b[y_at] = total.astype(BF16)
    copies_3 = []
    for k in range(1, NY):
        target = lax.rem(why + k, NY)
        copies_3.append(
            remote(half_b.at[target], recv_b2.at[k - 1], sem_y, NY - 2 + k, y_peers[k - 1])
        )
    for copy in copies_3:
        copy.start()
    for copy in copies_2:
        copy.wait_recv()
    total = half_a[zed].astype(F32)
    for k in range(NZ - 1):
        total = total + recv_a2[k].astype(F32)
    fin[0, :, :LANES_A] = total[:8]
    fin[1, :, :LANES_A] = total[8:]
    for copy in copies_3:
        copy.wait_recv()
    total = half_b[why].astype(F32)
    for k in range(NY - 1):
        total = total + recv_b2[k].astype(F32)
    fin[0, :, LANES_A:] = total[:8]
    fin[1, :, LANES_A:] = total[8:]
    swap = remote(fin.at[1 - core], fin_sib, sem_pair, 1, sibling)
    swap.start()
    swap.wait_recv()
    grads_out[core] = fin[core]
    grads_out[1 - core] = fin_sib[...]

    swap.wait_send()
    for copy in copies + copies_2 + copies_3:
        copy.wait_send()
    for sample in range(SAMPLES):
        for copy in out_halo(sample) + back_halo(sample):
            copy.wait_send()
        for copy in outputs(sample):
            copy.wait()

        @pl.when(jnp.logical_not(last))
        def _():
            edge_relay(sample).wait_send()
            node_relay(sample).wait_send()

        @pl.when(jnp.logical_not(first))
        def _():
            edge_return(sample).wait_send()
            node_return(sample).wait_send()


def local(
    node_in,
    edge_in,
    node_cot,
    edge_cot,
    send_rows,
    sender_row,
    receiver_row,
    edge_count,
    edge_w1,
    edge_w2,
    node_w1,
    node_w2,
    vectors,
):
    anywhere = pl.BlockSpec(memory_space=pl.ANY)
    vmem = pl.BlockSpec(memory_space=pltpu.VMEM)
    smem = pl.BlockSpec(memory_space=pltpu.SMEM)
    both = SAMPLES * ROWS

    def half(*shape):
        return pltpu.VMEM(shape, BF16)

    def full(*shape):
        return pltpu.VMEM(shape, F32)

    scratch = [
        half(3 * D, D),
        half(D, D),
        half(2 * D, D),
        half(D, D),
        full(8, D),
        half(2 * both, D),
        half(both, D),
        half(both, D),
        half(both, D),
        half(both, D),
        half(both, D),
        full(both, D),
        full(both, D),
        full(both, 128),
        half(both, D),
        half(both, D),
        full(both, D),
        full(both, D),
        full(both, 128),
        half(both, D),
        half(both, D),
        half(both, D),
        half(both, D),
        half(both, D),
        full(both, D),
        full(both, D),
        half(both, D),
        half(both, D),
        half(both, D),
        half(both, D),
        half(both, D),
        half(both, D),
        half(both, D),
        half(both, D),
        full(SAMPLES, 8, D),
        half(2, D, HALF),
        half(D, HALF),
        half(NZ, NY, 16, LANES_A),
        half(NZ, NY, 16, LANES_B),
        half(NY - 1, NZ, 16, LANES_A),
        half(NZ - 1, NY, 16, LANES_B),
        half(NZ, 16, LANES_A),
        half(NY, 16, LANES_B),
        half(NZ - 1, 16, LANES_A),
        half(NY - 1, 16, LANES_B),
        full(2, 8, HALF),
        full(8, HALF),
        pltpu.SemaphoreType.DMA((20,)),
        pltpu.SemaphoreType.DMA((2, 8)),
        pltpu.SemaphoreType.DMA((2, 8)),
        pltpu.SemaphoreType.DMA((2, 2)),
        pltpu.SemaphoreType.DMA((2, 6)),
        pltpu.SemaphoreType.DMA((2, 14)),
    ]
    shape = (1, SAMPLES, ROWS, D)
    node_out, edge_out, node_grad, edge_grad, grads = pl.pallas_call(
        kernel,
        out_shape=(
            jax.ShapeDtypeStruct(shape, BF16),
            jax.ShapeDtypeStruct(shape, BF16),
            jax.ShapeDtypeStruct(shape, F32),
            jax.ShapeDtypeStruct(shape, F32),
            jax.ShapeDtypeStruct((2, 8, HALF), F32),
        ),
        in_specs=[anywhere] * 4 + [vmem] * 3 + [smem] + [anywhere] * 4 + [vmem],
        out_specs=(anywhere,) * 4 + (vmem,),
        scratch_shapes=scratch,
        compiler_params=pltpu.CompilerParams(
            collective_id=0, has_side_effects=True, vmem_limit_bytes=48 << 20
        ),
        name="layers",
    )(
        node_in,
        edge_in,
        node_cot,
        edge_cot,
        send_rows.reshape(1, ROWS),
        sender_row.reshape(1, ROWS),
        receiver_row.reshape(1, ROWS),
        edge_count,
        edge_w1,
        edge_w2,
        node_w1,
        node_w2,
        vectors[0],
    )
    columns = jnp.concatenate([grads[0], grads[1]], 1).T
    return (
        node_out,
        edge_out,
        node_grad,
        edge_grad,
        columns[None, : 3 * D],
        columns[None, 3 * D : 4 * D],
        columns[None, 4 * D : 6 * D],
        columns[None, 6 * D : 7 * D],
        columns[None, 7 * D : 7 * D + 8],
    )


def solution(mesh):
    in_specs = (
        P("dp", "dom", None),
        P("dp", "dom", None),
        P("dp", "dom", None),
        P("dp", "dom", None),
        P("dom"),
        P("dom"),
        P("dom"),
        P("dom"),
        P("segment", None, None),
        P("segment", None, None),
        P("segment", None, None),
        P("segment", None, None),
        P("segment", None, None),
    )
    out_specs = (
        P("segment", "dp", "dom", None),
        P("segment", "dp", "dom", None),
        P("segment", "dp", "dom", None),
        P("segment", "dp", "dom", None),
        P("segment", None, ("dom", "dp")),
        P("segment", None, ("dom", "dp")),
        P("segment", None, ("dom", "dp")),
        P("segment", None, ("dom", "dp")),
        P("segment", None, ("dom", "dp")),
    )
    return jax.shard_map(local, mesh=mesh, in_specs=in_specs, out_specs=out_specs, check_vma=False)
```

```python
import functools

import jax
import jax.numpy as jnp
from jax import lax
from jax.experimental import pallas as pl
from jax.experimental.pallas import tpu as pltpu
from jax.sharding import PartitionSpec as P

F32 = jnp.float32
BF16 = jnp.bfloat16
MESH = pl.DeviceIdType.MESH

D = 512
ROWS = 128
HALO = 64
SAMPLES = 2
NY = 4
NZ = 8
DOMS = NY * NZ
SECTIONS = 4
HALF = 1920
LANES_A = 1280
LANES_B = HALF - LANES_A
CUT_A = 640
CUT_B = 384


def dot_nn(left, right):
    return jnp.dot(left, right, preferred_element_type=F32)


def dot_nt(left, right):
    return lax.dot_general(left, right, (((1,), (1,)), ((), ())), preferred_element_type=F32)


def sigmoid(values):
    return 0.5 * jnp.tanh(0.5 * values) + 0.5


def norm_parts(values):
    average = jnp.mean(values, -1, keepdims=True)
    centred = values - average
    scale = lax.rsqrt(jnp.mean(centred * centred, -1, keepdims=True) + 1e-05)
    return centred * scale, scale


def norm_back(cotangent, normed, scale):
    first = jnp.mean(cotangent, -1, keepdims=True)
    second = jnp.mean(cotangent * normed, -1, keepdims=True)
    return scale * (cotangent - first - normed * second)


def column_sum(values):
    return jnp.sum(values, 0, keepdims=True)


def kernel(
    node_in,
    edge_in,
    node_cot,
    edge_cot,
    send_rows_hbm,
    sender_row_hbm,
    receiver_row_hbm,
    edge_count,
    w1e_hbm,
    w2e_hbm,
    w1n_hbm,
    w2n_hbm,
    vectors_hbm,
    node_out,
    edge_out,
    node_grad,
    edge_grad,
    grads_out,
    w1e,
    w2e,
    w1n,
    w2n,
    send_rows,
    sender_row,
    receiver_row,
    vectors,
    coeffs,
    table,
    edge_x,
    node_x,
    snd,
    rcv,
    hid_e,
    pre_e,
    norm_e,
    scale_e,
    inc,
    hid_n,
    pre_n,
    norm_n,
    scale_n,
    node_o,
    edge_o,
    send_buf,
    d_node,
    d_edge,
    d_node_f,
    d_edge_f,
    d_node_h,
    d_edge_h,
    halo_back,
    ret,
    cot_pe,
    cot_le,
    cot_pn,
    cot_ln,
    vec_acc,
    grad_half,
    grad_sib,
    sum_a,
    sum_b,
    half_a,
    half_b,
    fold_ay,
    fold_bz,
    fold_az,
    fold_by,
    fin,
    fin_sib,
    sem_local,
    sem_relay,
    sem_halo,
    sem_pair,
    sem_y,
    sem_z,
):
    seg = lax.axis_index("segment")
    dom = lax.axis_index("dom")
    core = lax.axis_index("dp")
    zed = dom // NY
    why = dom % NY
    first = seg == 0
    last = seg == SECTIONS - 1
    ahead = lax.rem(seg + 1, SECTIONS)
    behind = lax.rem(seg + SECTIONS - 1, SECTIONS)
    dom_next = lax.rem(dom + 1, DOMS)
    dom_prev = lax.rem(dom + DOMS - 1, DOMS)
    y_at = [lax.rem(why + k, NY) for k in range(NY)]
    z_at = [lax.rem(zed + k, NZ) for k in range(NZ)]
    y_peer = [(seg, zed * NY + at, core) for at in y_at]
    z_peer = [(seg, at * NY + why, core) for at in z_at]
    sibling = (seg, dom, 1 - core)

    barrier = pltpu.get_barrier_semaphore()
    peers = [
        y_peer[1],
        y_peer[3],
        z_peer[1],
        z_peer[2],
        z_peer[6],
        z_peer[7],
        sibling,
        (ahead, dom, core),
        (behind, dom, core),
        (seg, dom_next, core),
        (seg, dom_prev, core),
    ]
    for peer in peers:
        pl.semaphore_signal(barrier, inc=1, device_id=peer, device_id_type=MESH)

    def local_copy(source, target, index):
        return pltpu.make_async_copy(source, target, sem_local.at[index])

    def span(sample):
        return pl.ds(sample * ROWS, ROWS)

    loads = [
        local_copy(w1e_hbm.at[0], w1e, 0),
        local_copy(w2e_hbm.at[0], w2e, 1),
        local_copy(w1n_hbm.at[0], w1n, 2),
        local_copy(w2n_hbm.at[0], w2n, 3),
    ]
    lists = [
        local_copy(send_rows_hbm, send_rows, 20),
        local_copy(sender_row_hbm, sender_row, 21),
        local_copy(receiver_row_hbm, receiver_row, 22),
        local_copy(vectors_hbm.at[0], vectors, 23),
    ]
    starts = []
    finals = []
    for sample in range(SAMPLES):
        starts.append(
            local_copy(node_in.at[sample], table.at[pl.ds(sample * 256, ROWS)], 4 + sample)
        )
        starts.append(local_copy(edge_in.at[sample], edge_x.at[span(sample)], 6 + sample))
        finals.append(local_copy(node_cot.at[sample], d_node.at[span(sample)], 8 + sample))
        finals.append(local_copy(edge_cot.at[sample], d_edge.at[span(sample)], 10 + sample))

    for copy in lists:
        copy.start()

    @pl.when(first)
    def _():
        for copy in starts:
            copy.start()

    for copy in loads:
        copy.start()

    @pl.when(last)
    def _():
        for copy in finals:
            copy.start()

    for copy in lists:
        copy.wait()
    slots = lax.broadcasted_iota(jnp.int32, (2 * ROWS, ROWS), 0)
    own = slots[:ROWS]
    send_t = (own == send_rows[...]).astype(F32)
    recv_t = (own == receiver_row[...]).astype(F32)
    pick_t = (slots == sender_row[...]).astype(F32)
    send_pick = send_t.T.astype(BF16)
    recv_pick = recv_t.T.astype(BF16)
    sender_pick = pick_t.T.astype(BF16)
    send_t = send_t.astype(BF16)
    recv_t = recv_t.astype(BF16)
    pick_t = pick_t.astype(BF16)
    live = (lax.broadcasted_iota(jnp.int32, (ROWS, 1), 0) < edge_count[0]).astype(F32)
    coeffs[...] = vectors[...].astype(F32)

    def coeff(row):
        return coeffs[row : row + 1, :]

    def remote(source, target, sems, index, peer):
        return pltpu.make_async_remote_copy(
            src_ref=source,
            dst_ref=target,
            send_sem=sems.at[0, index],
            recv_sem=sems.at[1, index],
            device_id=peer,
            device_id_type=MESH,
        )

    def halo_copies(source, sample, target_ref, base, kind):
        return (
            remote(
                source.at[pl.ds(sample * ROWS, HALO)],
                target_ref.at[pl.ds(base + HALO, HALO)],
                sem_halo,
                kind * 4 + sample * 2,
                (seg, dom_prev, core),
            ),
            remote(
                source.at[pl.ds(sample * ROWS + HALO, HALO)],
                target_ref.at[pl.ds(base, HALO)],
                sem_halo,
                kind * 4 + sample * 2 + 1,
                (seg, dom_next, core),
            ),
        )

    def out_halo(sample):
        return halo_copies(send_buf, sample, table, sample * 256 + ROWS, 0)

    def back_halo(sample):
        return halo_copies(halo_back, sample, ret, sample * ROWS, 1)

    def node_relay(sample):
        return remote(
            node_o.at[span(sample)],
            table.at[pl.ds(sample * 256, ROWS)],
            sem_relay,
            sample,
            (ahead, dom, core),
        )

    def edge_relay(sample):
        return remote(
            edge_o.at[span(sample)],
            edge_x.at[span(sample)],
            sem_relay,
            2 + sample,
            (ahead, dom, core),
        )

    def node_return(sample):
        return remote(
            d_node_h.at[span(sample)],
            d_node.at[span(sample)],
            sem_relay,
            4 + sample,
            (behind, dom, core),
        )

    def edge_return(sample):
        return remote(
            d_edge_h.at[span(sample)],
            d_edge.at[span(sample)],
            sem_relay,
            6 + sample,
            (behind, dom, core),
        )

    def outputs(sample):
        return (
            local_copy(node_o.at[span(sample)], node_out.at[0, sample], 12 + sample),
            local_copy(edge_o.at[span(sample)], edge_out.at[0, sample], 14 + sample),
        )

    def grad_outputs(sample):
        return (
            local_copy(d_node_f.at[span(sample)], node_grad.at[0, sample], 16 + sample),
            local_copy(d_edge_f.at[span(sample)], edge_grad.at[0, sample], 18 + sample),
        )

    pl.semaphore_wait(barrier, len(peers))

    def gather(sample):
        nodes = table[pl.ds(sample * 256, ROWS), :]
        send_buf[span(sample), :] = dot_nn(send_pick, nodes).astype(BF16)
        for copy in out_halo(sample):
            copy.start()
        node_x[span(sample), :] = nodes

    @pl.when(first)
    def _():
        for sample in range(SAMPLES):
            starts[2 * sample].wait()
            gather(sample)

    for sample in range(SAMPLES):
        rows = span(sample)
        if sample == 0:

            @pl.when(jnp.logical_not(first))
            def _():
                node_relay(0).wait_recv()
                gather(0)

            for copy in loads:
                copy.wait()
        nodes = node_x[rows, :]
        receivers = dot_nn(recv_pick, nodes).astype(BF16)
        rcv[rows, :] = receivers
        node_part = dot_nn(nodes, w1n[:D, :]) + coeff(4)
        edge_part = dot_nn(receivers, w1e[2 * D :, :]) + coeff(0)

        @pl.when(first)
        def _():
            starts[2 * sample + 1].wait()

        @pl.when(jnp.logical_not(first))
        def _():
            edge_relay(sample).wait_recv()

        edges = edge_x[rows, :]
        edge_part = edge_part + dot_nn(edges, w1e[:D, :])
        for copy in out_halo(sample):
            copy.wait_recv()
        senders = dot_nn(sender_pick, table[pl.ds(sample * 256, 256), :]).astype(BF16)
        snd[rows, :] = senders
        edge_pre = edge_part + dot_nn(senders, w1e[D : 2 * D, :])
        edge_hid = (edge_pre * sigmoid(edge_pre)).astype(BF16)
        pre_e[rows, :] = edge_pre
        hid_e[rows, :] = edge_hid
        edge_norm, edge_scale = norm_parts(dot_nn(edge_hid, w2e[...]) + coeff(1))
        norm_e[rows, :] = edge_norm
        scale_e[rows, :] = jnp.broadcast_to(edge_scale, (ROWS, 128))
        message = (edge_norm * coeff(2) + coeff(3)) * live
        edge_o[rows, :] = (edges.astype(F32) + message).astype(BF16)
        if sample == 0:

            @pl.when(jnp.logical_not(last))
            def _():
                edge_relay(0).start()

            @pl.when(jnp.logical_not(first))
            def _():
                node_relay(1).wait_recv()
                gather(1)

        incoming = dot_nn(recv_t, message.astype(BF16)).astype(BF16)
        inc[rows, :] = incoming
        node_pre = node_part + dot_nn(incoming, w1n[D:, :])
        node_hid = (node_pre * sigmoid(node_pre)).astype(BF16)
        pre_n[rows, :] = node_pre
        hid_n[rows, :] = node_hid
        node_norm, node_scale = norm_parts(dot_nn(node_hid, w2n[...]) + coeff(5))
        norm_n[rows, :] = node_norm
        scale_n[rows, :] = jnp.broadcast_to(node_scale, (ROWS, 128))
        node_o[rows, :] = (nodes.astype(F32) + node_norm * coeff(6) + coeff(7)).astype(BF16)

        @pl.when(jnp.logical_not(last))
        def _():
            node_relay(sample).start()
            if sample == 1:
                edge_relay(1).start()

        for copy in outputs(sample):
            copy.start()

    def silu_slope(values):
        gate = sigmoid(values)
        return gate * (1.0 + values * (1.0 - gate))

    for sample in range(SAMPLES):
        rows = span(sample)

        @pl.when(last)
        def _():
            finals[2 * sample].wait()

        @pl.when(jnp.logical_not(last))
        def _():
            node_return(sample).wait_recv()

        node_back = d_node[rows, :].astype(F32)
        node_norm = norm_n[rows, :]
        node_lin_back = norm_back(node_back * coeff(6), node_norm, scale_n[rows, 0:1])
        lin_half = node_lin_back.astype(BF16)
        cot_ln[rows, :] = lin_half
        node_pre_back = dot_nt(lin_half, w2n[...]).astype(BF16).astype(F32) * silu_slope(
            pre_n[rows, :]
        )
        pre_half = node_pre_back.astype(BF16)
        cot_pn[rows, :] = pre_half
        node_total = node_back + dot_nt(pre_half, w1n[:D, :]).astype(BF16).astype(F32)
        incoming_back = dot_nt(pre_half, w1n[D:, :]).astype(BF16)

        @pl.when(last)
        def _():
            finals[2 * sample + 1].wait()

        @pl.when(jnp.logical_not(last))
        def _():
            edge_return(sample).wait_recv()

        edge_back = d_edge[rows, :].astype(F32)
        edge_norm = norm_e[rows, :]
        message_back = (edge_back + dot_nn(recv_pick, incoming_back)) * live
        edge_lin_back = norm_back(message_back * coeff(2), edge_norm, scale_e[rows, 0:1])
        lin_half = edge_lin_back.astype(BF16)
        cot_le[rows, :] = lin_half
        edge_pre_back = dot_nt(lin_half, w2e[...]).astype(BF16).astype(F32) * silu_slope(
            pre_e[rows, :]
        )
        pre_half = edge_pre_back.astype(BF16)
        cot_pe[rows, :] = pre_half
        sender_back = dot_nt(pre_half, w1e[D : 2 * D, :]).astype(BF16)
        halo_back[rows, :] = dot_nn(pick_t[ROWS:, :], sender_back).astype(BF16)
        for copy in back_halo(sample):
            copy.start()
        edge_total = edge_back + dot_nt(pre_half, w1e[:D, :]).astype(BF16).astype(F32)
        d_edge_f[rows, :] = edge_total
        d_edge_h[rows, :] = edge_total.astype(BF16)

        @pl.when(jnp.logical_not(first))
        def _():
            edge_return(sample).start()

        receiver_back = dot_nt(pre_half, w1e[2 * D :, :]).astype(BF16)
        node_total = node_total + dot_nn(pick_t[:ROWS, :], sender_back).astype(BF16).astype(F32)
        node_total = node_total + dot_nn(recv_t, receiver_back).astype(BF16).astype(F32)
        sums = (
            edge_pre_back,
            edge_lin_back,
            message_back * edge_norm,
            message_back,
            node_pre_back,
            node_lin_back,
            node_back * node_norm,
            node_back,
        )
        for index, value in enumerate(sums):
            vec_acc[sample, index : index + 1, :] = column_sum(value)
        d_node_f[rows, :] = node_total

    def put(start, value):
        width = value.shape[1]
        here = value.astype(BF16)
        if start >= HALF:
            grad_half[1, :, start - HALF : start - HALF + width] = here
        elif start + width <= HALF:
            grad_half[0, :, start : start + width] = here
        else:
            cut = HALF - start
            grad_half[0, :, start:HALF] = here[:, :cut]
            grad_half[1, :, 0 : width - cut] = here[:, cut:]

    edge_pre_t = cot_pe[...].T
    put(0, dot_nn(edge_pre_t, edge_x[...]))
    put(D, dot_nn(edge_pre_t, snd[...]))
    put(2 * D, dot_nn(edge_pre_t, rcv[...]))
    put(3 * D, dot_nn(cot_le[...].T, hid_e[...]))
    node_pre_t = cot_pn[...].T
    put(4 * D, dot_nn(node_pre_t, node_x[...]))
    put(5 * D, dot_nn(node_pre_t, inc[...]))
    put(6 * D, dot_nn(cot_ln[...].T, hid_n[...]))
    vec_sum = vec_acc[0] + vec_acc[1]
    vec_block = jnp.concatenate([vec_sum, jnp.zeros((120, D), F32)], 0).T
    put(7 * D, jnp.concatenate([vec_block, jnp.zeros((D, 128), F32)], 1))

    pair = remote(grad_half.at[1 - core], grad_sib, sem_pair, 0, sibling)
    pair.start()
    for sample in range(SAMPLES):
        rows = span(sample)
        for copy in back_halo(sample):
            copy.wait_recv()
        node_total = d_node_f[rows, :] + dot_nn(send_t, ret[rows, :])
        d_node_f[rows, :] = node_total
        d_node_h[rows, :] = node_total.astype(BF16)

        @pl.when(jnp.logical_not(first))
        def _():
            node_return(sample).start()

        for copy in grad_outputs(sample):
            copy.start()

    pair.wait()
    for at in range(NZ):
        here = pl.ds(at * NY * 16, NY * 16)
        total = grad_half[core, here, :].astype(F32) + grad_sib[here, :].astype(F32)
        total = total.astype(BF16).reshape(NY, 16, HALF)
        sum_a[at] = total[:, :, :LANES_A]
        sum_b[at] = total[:, :, LANES_A:]

    def wide(ref):
        return ref[...].astype(F32)

    class YFold:
        def __init__(self, source, load, cut, parts, base):
            fold_p, fold_m, self.stage_p, self.stage_m, self.p0, self.p1, self.m0, self.m1 = parts
            low, high = slice(0, cut), slice(cut, None)
            self.load, self.low, self.high = load, low, high
            self.fold_p, self.fold_m = fold_p, fold_m

            def send(src, target, index, peer):
                return remote(src, target, sem_y, base + index, y_peer[peer])

            self.fp = send(source(y_at[2], low), fold_p, 0, 1)
            self.fm = send(source(y_at[2], high), fold_m, 1, 3)
            self.c_p1 = send(source(y_at[1], high), self.p1, 2, 1)
            self.c_m0 = send(source(y_at[3], low), self.m0, 3, 3)
            self.c_p0 = send(self.stage_p, self.p0, 4, 1)
            self.c_m1 = send(self.stage_m, self.m1, 5, 3)
            self.all = (self.fp, self.fm, self.c_p1, self.c_m0, self.c_p0, self.c_m1)

        def start(self):
            for copy in self.all[:4]:
                copy.start()

        def middle(self):
            self.fp.wait_recv()
            total = self.load(y_at[1], self.low).astype(F32) + wide(self.fold_p)
            self.stage_p[...] = total.astype(BF16)
            self.c_p0.start()
            self.fm.wait_recv()
            total = self.load(y_at[3], self.high).astype(F32) + wide(self.fold_m)
            self.stage_m[...] = total.astype(BF16)
            self.c_m1.start()

        def finish(self):
            for copy in self.all[2:]:
                copy.wait_recv()
            low = self.load(y_at[0], self.low).astype(F32) + wide(self.p0) + wide(self.m0)
            high = self.load(y_at[0], self.high).astype(F32) + wide(self.p1) + wide(self.m1)
            return low, high

    class ZFold:
        def __init__(self, source, cut, parts, base):
            self.r4p, self.r4m, self.r3p, self.r3m, self.r1p, self.r1m = parts[:6]
            self.stage_p, self.stage_m, self.r2p, self.r2m = parts[6:]
            self.source, self.cut = source, cut

            def send(src, target, index, peer):
                return remote(src, target, sem_z, base + index, z_peer[peer])

            far = source.at[z_at[4]]
            self.all = (
                send(far.at[..., :cut], self.r4p, 0, 2),
                send(far.at[..., cut:], self.r4m, 1, 6),
                send(source.at[z_at[3]], self.r3p, 2, 1),
                send(source.at[z_at[5]], self.r3m, 3, 7),
                send(source.at[z_at[1]], self.r1p, 4, 1),
                send(source.at[z_at[7]], self.r1m, 5, 7),
                send(self.stage_p, self.r2p, 6, 2),
                send(self.stage_m, self.r2m, 7, 6),
            )

        def start(self):
            for copy in self.all[:6]:
                copy.start()

        def middle(self):
            cut = self.cut
            self.all[2].wait_recv()
            self.all[0].wait_recv()
            total = self.source[z_at[2]].astype(F32) + wide(self.r3p)
            self.stage_p[..., cut:] = total[..., cut:].astype(BF16)
            self.stage_p[..., :cut] = (total[..., :cut] + wide(self.r4p)).astype(BF16)
            self.all[6].start()
            self.all[3].wait_recv()
            self.all[1].wait_recv()
            total = self.source[z_at[6]].astype(F32) + wide(self.r3m)
            self.stage_m[..., :cut] = total[..., :cut].astype(BF16)
            self.stage_m[..., cut:] = (total[..., cut:] + wide(self.r4m)).astype(BF16)
            self.all[7].start()

        def finish(self):
            for copy in self.all[4:]:
                copy.wait_recv()
            total = self.source[z_at[0]].astype(F32) + wide(self.r1p) + wide(self.r1m)
            return total + wide(self.r2p) + wide(self.r2m)

    a_y = YFold(
        lambda at, lanes: sum_a.at[:, at, :, lanes], lambda at, lanes: sum_a[:, at, :, lanes], CUT_A, fold_ay, 0
    )
    b_z = ZFold(sum_b, CUT_B, fold_bz, 0)
    a_z = ZFold(half_a, CUT_A, fold_az, 8)
    b_y = YFold(
        lambda at, lanes: half_b.at[at, :, lanes], lambda at, lanes: half_b[at, :, lanes], CUT_B, fold_by, 6
    )
    a_y.start()
    b_z.start()
    b_z.middle()
    a_y.middle()
    half_b[...] = b_z.finish().astype(BF16)
    b_y.start()
    low, high = a_y.finish()
    half_a[:, :, :CUT_A] = low.astype(BF16)
    half_a[:, :, CUT_A:] = high.astype(BF16)
    a_z.start()
    b_y.middle()
    low, high = b_y.finish()
    for index, rows in enumerate((slice(0, 8), slice(8, 16))):
        fin[index, :, LANES_A : LANES_A + CUT_B] = low[rows]
        fin[index, :, LANES_A + CUT_B :] = high[rows]
    a_z.middle()
    total = a_z.finish()
    fin[0, :, :LANES_A] = total[:8]
    fin[1, :, :LANES_A] = total[8:]
    swap = remote(fin.at[1 - core], fin_sib, sem_pair, 1, sibling)
    swap.start()
    swap.wait_recv()
    grads_out[core] = fin[core]
    grads_out[1 - core] = fin_sib[...]

    swap.wait_send()
    for copy in a_y.all + b_z.all + a_z.all + b_y.all:
        copy.wait_send()
    for sample in range(SAMPLES):
        for copy in out_halo(sample) + back_halo(sample):
            copy.wait_send()
        for copy in outputs(sample) + grad_outputs(sample):
            copy.wait()

        @pl.when(jnp.logical_not(last))
        def _():
            edge_relay(sample).wait_send()
            node_relay(sample).wait_send()

        @pl.when(jnp.logical_not(first))
        def _():
            edge_return(sample).wait_send()
            node_return(sample).wait_send()


def store_kernel(node_out, edge_out, node_grad, edge_grad, grads, *refs):
    results, held, rows_held, sems = refs[:9], refs[9:13], refs[13:18], refs[18]
    sources = (node_out, edge_out, node_grad, edge_grad)
    loads = [
        pltpu.make_async_copy(source, target, sems.at[index])
        for index, (source, target) in enumerate(zip(sources, held))
    ]
    stores = [
        pltpu.make_async_copy(source, target, sems.at[4 + index])
        for index, (source, target) in enumerate(zip(held + rows_held, results))
    ]
    for copy in loads:
        copy.start()
    w1e_rows, w2e_rows, w1n_rows, w2n_rows, vec_rows = rows_held
    w1e_rows[:, :] = grads[0, :, : 3 * D]
    w2e_rows[:, : HALF - 3 * D] = grads[0, :, 3 * D :]
    w2e_rows[:, HALF - 3 * D :] = grads[1, :, : 4 * D - HALF]
    w1n_rows[:, :] = grads[1, :, 4 * D - HALF : 6 * D - HALF]
    w2n_rows[:, :] = grads[1, :, 6 * D - HALF : 7 * D - HALF]
    columns = grads[1, :, 7 * D - HALF : 7 * D - HALF + 128].T
    vec_rows[...] = columns[:8, :]
    for copy in stores[4:]:
        copy.start()
    for load, copy in zip(loads, stores):
        load.wait()
        copy.start()
    for copy in stores:
        copy.wait()


def local(
    node_in,
    edge_in,
    node_cot,
    edge_cot,
    send_rows,
    sender_row,
    receiver_row,
    edge_count,
    edge_w1,
    edge_w2,
    node_w1,
    node_w2,
    vectors,
):
    anywhere = pl.BlockSpec(memory_space=pl.ANY)
    vmem = pl.BlockSpec(memory_space=pltpu.VMEM)
    smem = pl.BlockSpec(memory_space=pltpu.SMEM)
    both = SAMPLES * ROWS

    def half(*shape):
        return pltpu.VMEM(shape, BF16)

    def full(*shape):
        return pltpu.VMEM(shape, F32)

    def y_parts(lead, lanes, cut):
        low, high = half(*lead, cut), half(*lead, lanes - cut)
        return [low, high, low, high, low, high, low, high]

    def z_parts(lead, lanes, cut):
        return [half(*lead, cut), half(*lead, lanes - cut)] + [half(*lead, lanes)] * 8

    scratch = [
        half(3 * D, D),
        half(D, D),
        half(2 * D, D),
        half(D, D),
        pltpu.VMEM((1, ROWS), jnp.int32),
        pltpu.VMEM((1, ROWS), jnp.int32),
        pltpu.VMEM((1, ROWS), jnp.int32),
        half(8, D),
        full(8, D),
        half(2 * both, D),
        half(both, D),
        half(both, D),
        half(both, D),
        half(both, D),
        half(both, D),
        full(both, D),
        full(both, D),
        full(both, 128),
        half(both, D),
        half(both, D),
        full(both, D),
        full(both, D),
        full(both, 128),
        half(both, D),
        half(both, D),
        half(both, D),
        half(both, D),
        half(both, D),
        full(both, D),
        full(both, D),
        half(both, D),
        half(both, D),
        half(both, D),
        half(both, D),
        half(both, D),
        half(both, D),
        half(both, D),
        half(both, D),
        full(SAMPLES, 8, D),
        half(2, D, HALF),
        half(D, HALF),
        half(NZ, NY, 16, LANES_A),
        half(NZ, NY, 16, LANES_B),
        half(NZ, 16, LANES_A),
        half(NY, 16, LANES_B),
        y_parts((NZ, 16), LANES_A, CUT_A),
        z_parts((NY, 16), LANES_B, CUT_B),
        z_parts((16,), LANES_A, CUT_A),
        y_parts((16,), LANES_B, CUT_B),
        full(2, 8, HALF),
        full(8, HALF),
        pltpu.SemaphoreType.DMA((24,)),
        pltpu.SemaphoreType.DMA((2, 8)),
        pltpu.SemaphoreType.DMA((2, 8)),
        pltpu.SemaphoreType.DMA((2, 2)),
        pltpu.SemaphoreType.DMA((2, 12)),
        pltpu.SemaphoreType.DMA((2, 16)),
    ]
    shape = (1, SAMPLES, ROWS, D)
    node_out, edge_out, node_grad, edge_grad, grads = pl.pallas_call(
        kernel,
        out_shape=(
            jax.ShapeDtypeStruct(shape, BF16),
            jax.ShapeDtypeStruct(shape, BF16),
            jax.ShapeDtypeStruct(shape, F32),
            jax.ShapeDtypeStruct(shape, F32),
            jax.ShapeDtypeStruct((2, 8, HALF), F32),
        ),
        in_specs=[anywhere] * 7 + [smem] + [anywhere] * 5,
        out_specs=(anywhere,) * 4 + (vmem,),
        scratch_shapes=scratch,
        compiler_params=pltpu.CompilerParams(
            collective_id=0, has_side_effects=True, vmem_limit_bytes=60 << 20
        ),
        name="layers",
    )(
        node_in,
        edge_in,
        node_cot,
        edge_cot,
        send_rows.reshape(1, ROWS),
        sender_row.reshape(1, ROWS),
        receiver_row.reshape(1, ROWS),
        edge_count,
        edge_w1,
        edge_w2,
        node_w1,
        node_w2,
        vectors,
    )
    rows_of = (3 * D, D, 2 * D, D, 8)
    results = pl.pallas_call(
        store_kernel,
        out_shape=(
            jax.ShapeDtypeStruct(shape, BF16),
            jax.ShapeDtypeStruct(shape, BF16),
            jax.ShapeDtypeStruct(shape, F32),
            jax.ShapeDtypeStruct(shape, F32),
        )
        + tuple(jax.ShapeDtypeStruct((8, rows), F32) for rows in rows_of),
        in_specs=[anywhere] * 4 + [vmem],
        out_specs=(anywhere,) * 9,
        scratch_shapes=[pltpu.VMEM(shape, BF16)] * 2
        + [pltpu.VMEM(shape, F32)] * 2
        + [pltpu.VMEM((8, rows), F32) for rows in rows_of]
        + [pltpu.SemaphoreType.DMA((13,))],
        name="store",
    )(node_out, edge_out, node_grad, edge_grad, grads)
    return results[:4] + tuple(value.T[None] for value in results[4:8]) + (results[8][None],)


def solution(mesh):
    in_specs = (
        P("dp", "dom", None),
        P("dp", "dom", None),
        P("dp", "dom", None),
        P("dp", "dom", None),
        P("dom"),
        P("dom"),
        P("dom"),
        P("dom"),
        P("segment", None, None),
        P("segment", None, None),
        P("segment", None, None),
        P("segment", None, None),
        P("segment", None, None),
    )
    out_specs = (
        P("segment", "dp", "dom", None),
        P("segment", "dp", "dom", None),
        P("segment", "dp", "dom", None),
        P("segment", "dp", "dom", None),
        P("segment", None, ("dom", "dp")),
        P("segment", None, ("dom", "dp")),
        P("segment", None, ("dom", "dp")),
        P("segment", None, ("dom", "dp")),
        P("segment", None, ("dom", "dp")),
    )
    return jax.shard_map(local, mesh=mesh, in_specs=in_specs, out_specs=out_specs, check_vma=False)
```

```python
import functools

import jax
import jax.numpy as jnp
from jax import lax
from jax.experimental import pallas as pl
from jax.experimental.pallas import tpu as pltpu
from jax.sharding import PartitionSpec as P

F32 = jnp.float32
BF16 = jnp.bfloat16
MESH = pl.DeviceIdType.MESH

D = 512
ROWS = 128
HALO = 64
SAMPLES = 2
NY = 4
NZ = 8
DOMS = NY * NZ
SECTIONS = 4
HALF = 1920
LANES_A = 1152
LANES_B = HALF - LANES_A
CUT_A = 640
CUT_B = 384


def dot_nn(left, right):
    return jnp.dot(left, right, preferred_element_type=F32)


def dot_nt(left, right):
    return lax.dot_general(left, right, (((1,), (1,)), ((), ())), preferred_element_type=F32)


def sigmoid(values):
    return 0.5 * jnp.tanh(0.5 * values) + 0.5


def norm_parts(values):
    average = jnp.mean(values, -1, keepdims=True)
    centred = values - average
    scale = lax.rsqrt(jnp.mean(centred * centred, -1, keepdims=True) + 1e-05)
    return centred * scale, scale


def norm_back(cotangent, normed, scale):
    first = jnp.mean(cotangent, -1, keepdims=True)
    second = jnp.mean(cotangent * normed, -1, keepdims=True)
    return scale * (cotangent - first - normed * second)


def column_sum(values):
    return jnp.sum(values, 0, keepdims=True)


def kernel(
    node_in,
    edge_in,
    node_cot,
    edge_cot,
    send_rows_hbm,
    sender_row_hbm,
    receiver_row_hbm,
    edge_count,
    w1e_hbm,
    w2e_hbm,
    w1n_hbm,
    w2n_hbm,
    vectors_hbm,
    node_out,
    edge_out,
    node_grad,
    edge_grad,
    grads_out,
    w1e,
    w2e,
    w1n,
    w2n,
    send_rows,
    sender_row,
    receiver_row,
    vectors,
    coeffs,
    table,
    feats,
    feats_half,
    slope_e,
    norm_e,
    scale_e,
    slope_n,
    norm_n,
    scale_n,
    node_o,
    edge_o,
    send_buf,
    d_node,
    d_edge,
    d_node_f,
    d_edge_f,
    d_node_h,
    d_edge_h,
    halo_back,
    ret,
    cot_pe,
    cot_pn,
    sender_cot,
    cot_all,
    vec_acc,
    vec_sib,
    sum_a,
    sum_b,
    half_a,
    half_b,
    fold_ay,
    fold_bz,
    fold_az,
    fold_by,
    fin,
    fin_sib,
    sem_local,
    sem_relay,
    sem_halo,
    sem_pair,
    sem_y,
    sem_z,
):
    seg = lax.axis_index("segment")
    dom = lax.axis_index("dom")
    core = lax.axis_index("dp")
    zed = dom // NY
    why = dom % NY
    first = seg == 0
    last = seg == SECTIONS - 1
    ahead = lax.rem(seg + 1, SECTIONS)
    behind = lax.rem(seg + SECTIONS - 1, SECTIONS)
    dom_next = lax.rem(dom + 1, DOMS)
    dom_prev = lax.rem(dom + DOMS - 1, DOMS)
    y_at = [lax.rem(why + k, NY) for k in range(NY)]
    z_at = [lax.rem(zed + k, NZ) for k in range(NZ)]
    y_peer = [(seg, zed * NY + at, core) for at in y_at]
    z_peer = [(seg, at * NY + why, core) for at in z_at]
    sibling = (seg, dom, 1 - core)

    edge_x, snd, rcv, hid_e, node_x, inc, hid_n = [feats.at[index] for index in range(7)]

    barrier = pltpu.get_barrier_semaphore()
    peers = [
        y_peer[1],
        y_peer[3],
        z_peer[1],
        z_peer[2],
        z_peer[6],
        z_peer[7],
        sibling,
        (ahead, dom, core),
        (behind, dom, core),
        (seg, dom_next, core),
        (seg, dom_prev, core),
    ]
    for peer in peers:
        pl.semaphore_signal(barrier, inc=1, device_id=peer, device_id_type=MESH)

    def local_copy(source, target, index):
        return pltpu.make_async_copy(source, target, sem_local.at[index])

    def span(sample):
        return pl.ds(sample * ROWS, ROWS)

    loads = [
        local_copy(w1e_hbm.at[0], w1e, 0),
        local_copy(w2e_hbm.at[0], w2e, 1),
        local_copy(w1n_hbm.at[0], w1n, 2),
        local_copy(w2n_hbm.at[0], w2n, 3),
    ]
    lists = [
        local_copy(send_rows_hbm, send_rows, 20),
        local_copy(sender_row_hbm, sender_row, 21),
        local_copy(receiver_row_hbm, receiver_row, 22),
        local_copy(vectors_hbm.at[0], vectors, 23),
    ]
    starts = []
    finals = []
    for sample in range(SAMPLES):
        starts.append(
            local_copy(node_in.at[sample], table.at[pl.ds(sample * 256, ROWS)], 4 + sample)
        )
        starts.append(local_copy(edge_in.at[sample], edge_x.at[span(sample)], 6 + sample))
        finals.append(local_copy(node_cot.at[sample], d_node.at[span(sample)], 8 + sample))
        finals.append(local_copy(edge_cot.at[sample], d_edge.at[span(sample)], 10 + sample))

    for copy in lists:
        copy.start()

    @pl.when(first)
    def _():
        for copy in starts:
            copy.start()

    for copy in loads:
        copy.start()

    @pl.when(last)
    def _():
        for copy in finals:
            copy.start()

    for copy in lists:
        copy.wait()
    slots = lax.broadcasted_iota(jnp.int32, (2 * ROWS, ROWS), 0)
    own = slots[:ROWS]
    send_t = (own == send_rows[...]).astype(F32)
    recv_t = (own == receiver_row[...]).astype(F32)
    pick_t = (slots == sender_row[...]).astype(F32)
    send_pick = send_t.T.astype(BF16)
    recv_pick = recv_t.T.astype(BF16)
    sender_pick = pick_t.T.astype(BF16)
    send_t = send_t.astype(BF16)
    recv_t = recv_t.astype(BF16)
    pick_t = pick_t.astype(BF16)
    live = (lax.broadcasted_iota(jnp.int32, (ROWS, 1), 0) < edge_count[0]).astype(F32)
    coeffs[...] = vectors[...].astype(F32)

    def coeff(row):
        return coeffs[row : row + 1, :]

    def remote(source, target, sems, index, peer):
        return pltpu.make_async_remote_copy(
            src_ref=source,
            dst_ref=target,
            send_sem=sems.at[0, index],
            recv_sem=sems.at[1, index],
            device_id=peer,
            device_id_type=MESH,
        )

    def halo_copies(source, sample, target_ref, base, kind):
        return (
            remote(
                source.at[pl.ds(sample * ROWS, HALO)],
                target_ref.at[pl.ds(base + HALO, HALO)],
                sem_halo,
                kind * 4 + sample * 2,
                (seg, dom_prev, core),
            ),
            remote(
                source.at[pl.ds(sample * ROWS + HALO, HALO)],
                target_ref.at[pl.ds(base, HALO)],
                sem_halo,
                kind * 4 + sample * 2 + 1,
                (seg, dom_next, core),
            ),
        )

    def out_halo(sample):
        return halo_copies(send_buf, sample, table, sample * 256 + ROWS, 0)

    def back_halo(sample):
        return halo_copies(halo_back, sample, ret, sample * ROWS, 1)

    def node_relay(sample):
        return remote(
            node_o.at[span(sample)],
            table.at[pl.ds(sample * 256, ROWS)],
            sem_relay,
            sample,
            (ahead, dom, core),
        )

    def edge_relay(sample):
        return remote(
            edge_o.at[span(sample)],
            edge_x.at[span(sample)],
            sem_relay,
            2 + sample,
            (ahead, dom, core),
        )

    def node_return(sample):
        return remote(
            d_node_h.at[span(sample)],
            d_node.at[span(sample)],
            sem_relay,
            4 + sample,
            (behind, dom, core),
        )

    def edge_return(sample):
        return remote(
            d_edge_h.at[span(sample)],
            d_edge.at[span(sample)],
            sem_relay,
            6 + sample,
            (behind, dom, core),
        )

    def outputs(sample):
        return (
            local_copy(node_o.at[span(sample)], node_out.at[0, sample], 12 + sample),
            local_copy(edge_o.at[span(sample)], edge_out.at[0, sample], 14 + sample),
        )

    def grad_outputs(sample):
        return (
            local_copy(d_node_f.at[span(sample)], node_grad.at[0, sample], 16 + sample),
            local_copy(d_edge_f.at[span(sample)], edge_grad.at[0, sample], 18 + sample),
        )

    pl.semaphore_wait(barrier, len(peers))

    def lanes_of(side):
        return pl.ds(pl.multiple_of(side * (D // 2), D // 2), D // 2)

    own_feats = local_copy(
        feats.at[:, :, lanes_of(core)], feats_half.at[:, pl.ds(0, SAMPLES * ROWS)], 24
    )
    pair_feats = remote(
        feats.at[:, :, lanes_of(1 - core)],
        feats_half.at[:, pl.ds(SAMPLES * ROWS, SAMPLES * ROWS)],
        sem_pair,
        0,
        sibling,
    )
    pair_vec = remote(vec_acc, vec_sib, sem_pair, 4, sibling)

    def pair_cots(sample):
        return remote(
            cot_all.at[:, :, pl.ds(sample * ROWS, ROWS)],
            cot_all.at[:, :, pl.ds((SAMPLES + sample) * ROWS, ROWS)],
            sem_pair,
            2 + sample,
            sibling,
        )

    def either(at_last, when_last, when_not):
        if at_last is None:
            pl.when(last)(when_last)
            pl.when(jnp.logical_not(last))(when_not)
        elif at_last:
            when_last()
        else:
            when_not()

    def backward_main(sample, at_last):
        rows = span(sample)

        either(
            at_last,
            lambda: finals[2 * sample].wait(),
            lambda: node_return(sample).wait_recv(),
        )

        node_back = d_node[rows, :].astype(F32)
        node_norm = norm_n[rows, :]
        node_lin_back = norm_back(node_back * coeff(6), node_norm, scale_n[rows, 0:1])
        lin_half = node_lin_back.astype(BF16)
        node_lin_half = lin_half
        node_pre_back = dot_nt(lin_half, w2n[...]).astype(BF16).astype(F32) * slope_n[rows, :]
        pre_half = node_pre_back.astype(BF16)
        cot_pn[rows, :] = pre_half
        node_pre_half = pre_half
        incoming_back = dot_nt(pre_half, w1n[D:, :]).astype(BF16)

        either(
            at_last,
            lambda: finals[2 * sample + 1].wait(),
            lambda: edge_return(sample).wait_recv(),
        )

        edge_back = d_edge[rows, :].astype(F32)
        edge_norm = norm_e[rows, :]
        message_back = (edge_back + dot_nn(recv_pick, incoming_back)) * live
        edge_lin_back = norm_back(message_back * coeff(2), edge_norm, scale_e[rows, 0:1])
        lin_half = edge_lin_back.astype(BF16)
        edge_lin_half = lin_half
        edge_pre_back = dot_nt(lin_half, w2e[...]).astype(BF16).astype(F32) * slope_e[rows, :]
        pre_half = edge_pre_back.astype(BF16)
        cot_pe[rows, :] = pre_half
        sender_back = dot_nt(pre_half, w1e[D : 2 * D, :]).astype(BF16)
        halo_back[rows, :] = dot_nn(pick_t[ROWS:, :], sender_back).astype(BF16)
        for copy in back_halo(sample):
            copy.start()
        sender_cot[rows, :] = sender_back
        for index, value in enumerate((pre_half, edge_lin_half, node_pre_half, node_lin_half)):
            cot_all[index, :, sample * ROWS : (sample + 1) * ROWS] = value.T
        pair_cots(sample).start()
        sums = (
            edge_pre_back,
            edge_lin_back,
            message_back * edge_norm,
            message_back,
            node_pre_back,
            node_lin_back,
            node_back * node_norm,
            node_back,
        )
        for index, value in enumerate(sums):
            vec_acc[sample, index : index + 1, :] = column_sum(value)
        if sample == 1:
            pair_vec.start()
        edge_total = edge_back + dot_nt(pre_half, w1e[:D, :]).astype(BF16).astype(F32)
        d_edge_f[rows, :] = edge_total
        d_edge_h[rows, :] = edge_total.astype(BF16)

        @pl.when(jnp.logical_not(first))
        def _():
            edge_return(sample).start()

    def backward_rest(sample):
        rows = span(sample)
        node_total = d_node[rows, :].astype(F32)
        node_total = node_total + dot_nt(cot_pn[rows, :], w1n[:D, :]).astype(BF16).astype(F32)
        receiver_back = dot_nt(cot_pe[rows, :], w1e[2 * D :, :]).astype(BF16)
        node_total = node_total + dot_nn(pick_t[:ROWS, :], sender_cot[rows, :]).astype(
            BF16
        ).astype(F32)
        node_total = node_total + dot_nn(recv_t, receiver_back).astype(BF16).astype(F32)
        d_node_f[rows, :] = node_total

    def finish(sample):
        rows = span(sample)
        for copy in back_halo(sample):
            copy.wait_recv()
        node_total = d_node_f[rows, :] + dot_nn(send_t, ret[rows, :])
        d_node_f[rows, :] = node_total
        d_node_h[rows, :] = node_total.astype(BF16)

        @pl.when(jnp.logical_not(first))
        def _():
            node_return(sample).start()

        for copy in grad_outputs(sample):
            copy.start()

    def gather(sample):
        nodes = table[pl.ds(sample * 256, ROWS), :]
        send_buf[span(sample), :] = dot_nn(send_pick, nodes).astype(BF16)
        for copy in out_halo(sample):
            copy.start()
        node_x[span(sample), :] = nodes

    @pl.when(first)
    def _():
        for sample in range(SAMPLES):
            starts[2 * sample].wait()
            gather(sample)

    for sample in range(SAMPLES):
        rows = span(sample)
        if sample == 0:

            @pl.when(jnp.logical_not(first))
            def _():
                node_relay(0).wait_recv()
                gather(0)

            for copy in loads:
                copy.wait()
        nodes = node_x[rows, :]
        receivers = dot_nn(recv_pick, nodes).astype(BF16)
        rcv[rows, :] = receivers
        node_part = dot_nn(nodes, w1n[:D, :]) + coeff(4)
        edge_part = dot_nn(receivers, w1e[2 * D :, :]) + coeff(0)

        @pl.when(first)
        def _():
            starts[2 * sample + 1].wait()

        @pl.when(jnp.logical_not(first))
        def _():
            edge_relay(sample).wait_recv()

        edges = edge_x[rows, :]
        edge_part = edge_part + dot_nn(edges, w1e[:D, :])
        if sample == 0:

            @pl.when(jnp.logical_not(first))
            def _():
                node_relay(1).wait_recv()
                gather(1)

        for copy in out_halo(sample):
            copy.wait_recv()
        senders = dot_nn(sender_pick, table[pl.ds(sample * 256, 256), :]).astype(BF16)
        snd[rows, :] = senders
        edge_pre = edge_part + dot_nn(senders, w1e[D : 2 * D, :])
        edge_gate = sigmoid(edge_pre)
        edge_hid = (edge_pre * edge_gate).astype(BF16)
        hid_e[rows, :] = edge_hid
        edge_norm, edge_scale = norm_parts(dot_nn(edge_hid, w2e[...]) + coeff(1))
        norm_e[rows, :] = edge_norm
        scale_e[rows, :] = jnp.broadcast_to(edge_scale, (ROWS, 128))
        message = (edge_norm * coeff(2) + coeff(3)) * live
        edge_o[rows, :] = (edges.astype(F32) + message).astype(BF16)
        if sample == 0:

            @pl.when(jnp.logical_not(last))
            def _():
                edge_relay(0).start()

        incoming = dot_nn(recv_t, message.astype(BF16)).astype(BF16)
        inc[rows, :] = incoming
        node_pre = node_part + dot_nn(incoming, w1n[D:, :])
        node_gate = sigmoid(node_pre)
        node_hid = (node_pre * node_gate).astype(BF16)
        hid_n[rows, :] = node_hid
        node_norm, node_scale = norm_parts(dot_nn(node_hid, w2n[...]) + coeff(5))
        norm_n[rows, :] = node_norm
        scale_n[rows, :] = jnp.broadcast_to(node_scale, (ROWS, 128))
        node_o[rows, :] = (nodes.astype(F32) + node_norm * coeff(6) + coeff(7)).astype(BF16)

        @pl.when(jnp.logical_not(last))
        def _():
            node_relay(sample).start()

        for copy in outputs(sample):
            copy.start()
        slope_e[rows, :] = edge_gate * (1.0 + edge_pre * (1.0 - edge_gate))
        slope_n[rows, :] = node_gate * (1.0 + node_pre * (1.0 - node_gate))
        if sample == 0:

            @pl.when(last)
            def _():
                backward_main(0, True)
                backward_rest(0)

    @pl.when(jnp.logical_not(last))
    def _():
        node_relay(1).wait_send()
        edge_relay(1).start()

    own_feats.start()
    pair_feats.start()

    @pl.when(jnp.logical_not(last))
    def _():
        backward_main(0, False)
        backward_rest(0)

    finish(0)
    backward_main(1, None)

    def wide(ref):
        return ref[...].astype(F32)

    class YFold:
        def __init__(self, source, load, cut, parts, base):
            fold_p, fold_m, self.stage_p, self.stage_m, self.p0, self.p1, self.m0, self.m1 = parts
            low, high = slice(0, cut), slice(cut, None)
            self.load, self.low, self.high = load, low, high
            self.fold_p, self.fold_m = fold_p, fold_m

            def send(src, target, index, peer):
                return remote(src, target, sem_y, base + index, y_peer[peer])

            self.fp = send(source(y_at[2], low), fold_p, 0, 1)
            self.fm = send(source(y_at[2], high), fold_m, 1, 3)
            self.c_p1 = send(source(y_at[1], high), self.p1, 2, 1)
            self.c_m0 = send(source(y_at[3], low), self.m0, 3, 3)
            self.c_p0 = send(self.stage_p, self.p0, 4, 1)
            self.c_m1 = send(self.stage_m, self.m1, 5, 3)
            self.all = (self.fp, self.fm, self.c_p1, self.c_m0, self.c_p0, self.c_m1)

        def start(self):
            for copy in self.all[:4]:
                copy.start()

        def middle(self):
            self.fp.wait_recv()
            total = self.load(y_at[1], self.low).astype(F32) + wide(self.fold_p)
            self.stage_p[...] = total.astype(BF16)
            self.c_p0.start()
            self.fm.wait_recv()
            total = self.load(y_at[3], self.high).astype(F32) + wide(self.fold_m)
            self.stage_m[...] = total.astype(BF16)
            self.c_m1.start()

        def finish(self):
            for copy in self.all[2:]:
                copy.wait_recv()
            low = self.load(y_at[0], self.low).astype(F32) + wide(self.p0) + wide(self.m0)
            high = self.load(y_at[0], self.high).astype(F32) + wide(self.p1) + wide(self.m1)
            return low, high

    class ZFold:
        def __init__(self, source, cut, parts, base):
            self.r4p, self.r4m, self.r3p, self.r3m, self.r1p, self.r1m = parts[:6]
            self.stage_p, self.stage_m, self.r2p, self.r2m = parts[6:]
            self.source, self.cut = source, cut

            def send(src, target, index, peer):
                return remote(src, target, sem_z, base + index, z_peer[peer])

            far = source.at[z_at[4]]
            self.all = (
                send(far.at[..., :cut], self.r4p, 0, 2),
                send(far.at[..., cut:], self.r4m, 1, 6),
                send(source.at[z_at[3]], self.r3p, 2, 1),
                send(source.at[z_at[5]], self.r3m, 3, 7),
                send(source.at[z_at[1]], self.r1p, 4, 1),
                send(source.at[z_at[7]], self.r1m, 5, 7),
                send(self.stage_p, self.r2p, 6, 2),
                send(self.stage_m, self.r2m, 7, 6),
            )

        def start(self):
            for copy in self.all[:6]:
                copy.start()

        def middle(self):
            cut = self.cut
            self.all[2].wait_recv()
            self.all[0].wait_recv()
            total = self.source[z_at[2]].astype(F32) + wide(self.r3p)
            self.stage_p[..., cut:] = total[..., cut:].astype(BF16)
            self.stage_p[..., :cut] = (total[..., :cut] + wide(self.r4p)).astype(BF16)
            self.all[6].start()
            self.all[3].wait_recv()
            self.all[1].wait_recv()
            total = self.source[z_at[6]].astype(F32) + wide(self.r3m)
            self.stage_m[..., :cut] = total[..., :cut].astype(BF16)
            self.stage_m[..., cut:] = (total[..., cut:] + wide(self.r4m)).astype(BF16)
            self.all[7].start()

        def finish(self):
            for copy in self.all[4:]:
                copy.wait_recv()
            total = self.source[z_at[0]].astype(F32) + wide(self.r1p) + wide(self.r1m)
            return total + wide(self.r2p) + wide(self.r2m)

    a_y = YFold(
        lambda at, lanes: sum_a.at[:, at, :, lanes], lambda at, lanes: sum_a[:, at, :, lanes], CUT_A, fold_ay, 0
    )
    b_z = ZFold(sum_b, CUT_B, fold_bz, 0)
    a_z = ZFold(half_a, CUT_A, fold_az, 8)
    b_y = YFold(
        lambda at, lanes: half_b.at[at, :, lanes], lambda at, lanes: half_b[at, :, lanes], CUT_B, fold_by, 6
    )
    own_feats.wait()
    pair_feats.wait_recv()
    for sample in range(SAMPLES):
        pair_cots(sample).wait_recv()

    def spread(value):
        return value.astype(BF16).reshape(NZ, NY, 16, value.shape[1])

    width = D // 2
    for index, which in enumerate((2, 2, 3)):
        value = dot_nn(cot_all[which], feats_half[4 + index])
        sum_b[:, :, :, index * width : (index + 1) * width] = spread(value)
    pl.when(first)(b_z.start)
    for index, which in enumerate((0, 0, 0, 1)):
        value = dot_nn(cot_all[which], feats_half[index])
        sum_a[:, :, :, index * width : (index + 1) * width] = spread(value)
    pair_vec.wait_recv()
    vec_sum = vec_acc[0] + vec_acc[1] + vec_sib[0] + vec_sib[1]
    vec_block = jnp.concatenate([vec_sum, jnp.zeros((120, D), F32)], 0).T
    sum_a[:, :, :, 4 * width :] = spread(vec_block)
    pl.when(first)(a_y.start)
    backward_rest(1)
    finish(1)

    @pl.when(jnp.logical_not(first))
    def _():
        b_z.start()
        a_y.start()

    a_y.middle()
    b_z.middle()
    low, high = a_y.finish()
    half_a[:, :, :CUT_A] = low.astype(BF16)
    half_a[:, :, CUT_A:] = high.astype(BF16)
    a_z.start()
    half_b[...] = b_z.finish().astype(BF16)
    b_y.start()
    b_y.middle()
    a_z.middle()
    low, high = b_y.finish()
    for index, rows in enumerate((slice(0, 8), slice(8, 16))):
        fin[index, :, LANES_A : LANES_A + CUT_B] = low[rows]
        fin[index, :, LANES_A + CUT_B :] = high[rows]
    total = a_z.finish()
    fin[0, :, :LANES_A] = total[:8]
    fin[1, :, :LANES_A] = total[8:]
    swap = remote(fin.at[1 - core], fin_sib, sem_pair, 1, sibling)
    swap.start()
    swap.wait_recv()
    grads_out[core] = fin[core]
    grads_out[1 - core] = fin_sib[...]

    swap.wait_send()
    pair_feats.wait_send()
    pair_vec.wait_send()
    for sample in range(SAMPLES):
        pair_cots(sample).wait_send()
    for copy in a_y.all + b_z.all + a_z.all + b_y.all:
        copy.wait_send()
    for sample in range(SAMPLES):
        for copy in out_halo(sample) + back_halo(sample):
            copy.wait_send()
        for copy in outputs(sample) + grad_outputs(sample):
            copy.wait()

        @pl.when(jnp.logical_not(last))
        def _():
            edge_relay(sample).wait_send()
            if sample == 0:
                node_relay(0).wait_send()

        @pl.when(jnp.logical_not(first))
        def _():
            edge_return(sample).wait_send()
            node_return(sample).wait_send()


def store_kernel(node_out, edge_out, node_grad, edge_grad, grads_hbm, *refs):
    results, held, rows_held, grads, sems = refs[:9], refs[9:13], refs[13:18], refs[18], refs[19]
    grads_load = pltpu.make_async_copy(grads_hbm, grads, sems.at[13])
    grads_load.start()
    sources = (node_out, edge_out, node_grad, edge_grad)
    loads = [
        pltpu.make_async_copy(source, target, sems.at[index])
        for index, (source, target) in enumerate(zip(sources, held))
    ]
    stores = [
        pltpu.make_async_copy(source, target, sems.at[4 + index])
        for index, (source, target) in enumerate(zip(held + rows_held, results))
    ]
    for copy in loads:
        copy.start()
    w1e_rows, w2e_rows, w1n_rows, w2n_rows, vec_rows = rows_held
    grads_load.wait()
    width = D // 2
    places = [(w1e_rows, 0), (w1e_rows, D), (w1e_rows, 2 * D), (w2e_rows, 0)]
    places += [(w1n_rows, 0), (w1n_rows, D), (w2n_rows, 0)]
    for index, (target, start) in enumerate(places):
        lane = index * width if index < 4 else LANES_A + (index - 4) * width
        for side in range(2):
            target[:, start + side * width : start + (side + 1) * width] = grads[
                side, :, lane : lane + width
            ]
    columns = grads[0, :, 4 * width : 4 * width + 128].T
    vec_rows[...] = columns[:8, :]
    for copy in stores[4:]:
        copy.start()
    for load, copy in zip(loads, stores):
        load.wait()
        copy.start()
    for copy in stores:
        copy.wait()


def local(
    node_in,
    edge_in,
    node_cot,
    edge_cot,
    send_rows,
    sender_row,
    receiver_row,
    edge_count,
    edge_w1,
    edge_w2,
    node_w1,
    node_w2,
    vectors,
):
    anywhere = pl.BlockSpec(memory_space=pl.ANY)
    vmem = pl.BlockSpec(memory_space=pltpu.VMEM)
    smem = pl.BlockSpec(memory_space=pltpu.SMEM)
    both = SAMPLES * ROWS

    def half(*shape):
        return pltpu.VMEM(shape, BF16)

    def full(*shape):
        return pltpu.VMEM(shape, F32)

    def y_parts(lead, lanes, cut):
        low, high = half(*lead, cut), half(*lead, lanes - cut)
        return [low, high, low, high, low, high, low, high]

    def z_parts(lead, lanes, cut):
        return [half(*lead, cut), half(*lead, lanes - cut)] + [half(*lead, lanes)] * 8

    scratch = [
        half(3 * D, D),
        half(D, D),
        half(2 * D, D),
        half(D, D),
        pltpu.VMEM((1, ROWS), jnp.int32),
        pltpu.VMEM((1, ROWS), jnp.int32),
        pltpu.VMEM((1, ROWS), jnp.int32),
        half(8, D),
        full(8, D),
        half(2 * both, D),
        half(7, both, D),
        half(7, 2 * both, D // 2),
        full(both, D),
        full(both, D),
        full(both, 128),
        full(both, D),
        full(both, D),
        full(both, 128),
        half(both, D),
        half(both, D),
        half(both, D),
        half(both, D),
        half(both, D),
        full(both, D),
        full(both, D),
        half(both, D),
        half(both, D),
        half(both, D),
        half(both, D),
        half(both, D),
        half(both, D),
        half(both, D),
        half(4, D, 2 * both),
        full(SAMPLES, 8, D),
        full(SAMPLES, 8, D),
        half(NZ, NY, 16, LANES_A),
        half(NZ, NY, 16, LANES_B),
        half(NZ, 16, LANES_A),
        half(NY, 16, LANES_B),
        y_parts((NZ, 16), LANES_A, CUT_A),
        z_parts((NY, 16), LANES_B, CUT_B),
        z_parts((16,), LANES_A, CUT_A),
        y_parts((16,), LANES_B, CUT_B),
        full(2, 8, HALF),
        full(8, HALF),
        pltpu.SemaphoreType.DMA((25,)),
        pltpu.SemaphoreType.DMA((2, 8)),
        pltpu.SemaphoreType.DMA((2, 8)),
        pltpu.SemaphoreType.DMA((2, 5)),
        pltpu.SemaphoreType.DMA((2, 12)),
        pltpu.SemaphoreType.DMA((2, 16)),
    ]
    shape = (1, SAMPLES, ROWS, D)
    node_out, edge_out, node_grad, edge_grad, grads = pl.pallas_call(
        kernel,
        out_shape=(
            jax.ShapeDtypeStruct(shape, BF16),
            jax.ShapeDtypeStruct(shape, BF16),
            jax.ShapeDtypeStruct(shape, F32),
            jax.ShapeDtypeStruct(shape, F32),
            jax.ShapeDtypeStruct((2, 8, HALF), F32),
        ),
        in_specs=[anywhere] * 7 + [smem] + [anywhere] * 5,
        out_specs=(anywhere,) * 4 + (vmem,),
        scratch_shapes=scratch,
        compiler_params=pltpu.CompilerParams(
            collective_id=0, has_side_effects=True, vmem_limit_bytes=60 << 20
        ),
        name="layers",
    )(
        node_in,
        edge_in,
        node_cot,
        edge_cot,
        send_rows.reshape(1, ROWS),
        sender_row.reshape(1, ROWS),
        receiver_row.reshape(1, ROWS),
        edge_count,
        edge_w1,
        edge_w2,
        node_w1,
        node_w2,
        vectors,
    )
    rows_of = (3 * D, D, 2 * D, D, 8)
    results = pl.pallas_call(
        store_kernel,
        out_shape=(
            jax.ShapeDtypeStruct(shape, BF16),
            jax.ShapeDtypeStruct(shape, BF16),
            jax.ShapeDtypeStruct(shape, F32),
            jax.ShapeDtypeStruct(shape, F32),
        )
        + tuple(jax.ShapeDtypeStruct((8, rows), F32) for rows in rows_of),
        in_specs=[anywhere] * 5,
        out_specs=(anywhere,) * 9,
        scratch_shapes=[pltpu.VMEM(shape, BF16)] * 2
        + [pltpu.VMEM(shape, F32)] * 2
        + [pltpu.VMEM((8, rows), F32) for rows in rows_of]
        + [pltpu.VMEM((2, 8, HALF), F32), pltpu.SemaphoreType.DMA((14,))],
        name="store",
    )(node_out, edge_out, node_grad, edge_grad, grads)
    return results[:4] + tuple(value.T[None] for value in results[4:8]) + (results[8][None],)


def solution(mesh):
    in_specs = (
        P("dp", "dom", None),
        P("dp", "dom", None),
        P("dp", "dom", None),
        P("dp", "dom", None),
        P("dom"),
        P("dom"),
        P("dom"),
        P("dom"),
        P("segment", None, None),
        P("segment", None, None),
        P("segment", None, None),
        P("segment", None, None),
        P("segment", None, None),
    )
    out_specs = (
        P("segment", "dp", "dom", None),
        P("segment", "dp", "dom", None),
        P("segment", "dp", "dom", None),
        P("segment", "dp", "dom", None),
        P("segment", None, ("dom", "dp")),
        P("segment", None, ("dom", "dp")),
        P("segment", None, ("dom", "dp")),
        P("segment", None, ("dom", "dp")),
        P("segment", None, ("dom", "dp")),
    )
    return jax.shard_map(local, mesh=mesh, in_specs=in_specs, out_specs=out_specs, check_vma=False)
```

```python
import functools

import jax
import jax.numpy as jnp
from jax import lax
from jax.experimental import pallas as pl
from jax.experimental.pallas import tpu as pltpu
from jax.sharding import PartitionSpec as P

F32 = jnp.float32
BF16 = jnp.bfloat16
MESH = pl.DeviceIdType.MESH

D = 512
ROWS = 128
HALO = 64
SAMPLES = 2
NY = 4
NZ = 8
DOMS = NY * NZ
SECTIONS = 4
HALF = 1920
LANES_A = 512
LANES_V = 640
LANES_B = HALF - LANES_A - LANES_V
CUT_A = 256
CUT_V = 384
CUT_B = 384


def dot_nn(left, right):
    return jnp.dot(left, right, preferred_element_type=F32)


def dot_nt(left, right):
    return lax.dot_general(left, right, (((1,), (1,)), ((), ())), preferred_element_type=F32)


def sigmoid(values):
    return 0.5 * jnp.tanh(0.5 * values) + 0.5


def norm_parts(values):
    average = jnp.mean(values, -1, keepdims=True)
    centred = values - average
    scale = lax.rsqrt(jnp.mean(centred * centred, -1, keepdims=True) + 1e-05)
    return centred * scale, scale


def norm_back(cotangent, normed, scale):
    first = jnp.mean(cotangent, -1, keepdims=True)
    second = jnp.mean(cotangent * normed, -1, keepdims=True)
    return scale * (cotangent - first - normed * second)


def column_sum(values):
    return jnp.sum(values, 0, keepdims=True)


def kernel(
    node_in,
    edge_in,
    node_cot,
    edge_cot,
    send_rows_hbm,
    sender_row_hbm,
    receiver_row_hbm,
    edge_count,
    w1e_hbm,
    w2e_hbm,
    w1n_hbm,
    w2n_hbm,
    vectors_hbm,
    node_out,
    edge_out,
    node_grad,
    edge_grad,
    grads_out,
    w1e,
    w2e,
    w1n,
    w2n,
    send_rows,
    sender_row,
    receiver_row,
    vectors,
    coeffs,
    table,
    feats,
    feats_half,
    slope_e,
    norm_e,
    scale_e,
    slope_n,
    norm_n,
    scale_n,
    node_o,
    edge_o,
    send_buf,
    d_node,
    d_edge,
    d_node_f,
    d_edge_f,
    d_node_h,
    d_edge_h,
    halo_back,
    ret,
    cot_pe,
    cot_pn,
    sender_cot,
    cot_all,
    vec_acc,
    vec_sib,
    sum_a,
    sum_v,
    sum_b,
    half_a,
    half_v,
    half_b,
    fold_ay,
    fold_vy,
    fold_bz,
    fold_az,
    fold_vz,
    recv_by,
    fin,
    fin_sib,
    sem_local,
    sem_relay,
    sem_halo,
    sem_pair,
    sem_y,
    sem_z,
):
    seg = lax.axis_index("segment")
    dom = lax.axis_index("dom")
    core = lax.axis_index("dp")
    zed = dom // NY
    why = dom % NY
    first = seg == 0
    last = seg == SECTIONS - 1
    ahead = lax.rem(seg + 1, SECTIONS)
    behind = lax.rem(seg + SECTIONS - 1, SECTIONS)
    dom_next = lax.rem(dom + 1, DOMS)
    dom_prev = lax.rem(dom + DOMS - 1, DOMS)
    y_at = [lax.rem(why + k, NY) for k in range(NY)]
    z_at = [lax.rem(zed + k, NZ) for k in range(NZ)]
    y_peer = [(seg, zed * NY + at, core) for at in y_at]
    z_peer = [(seg, at * NY + why, core) for at in z_at]
    sibling = (seg, dom, 1 - core)

    edge_x, snd, rcv, hid_e, node_x, inc, hid_n = [feats.at[index] for index in range(7)]

    barrier = pltpu.get_barrier_semaphore()
    peers = [
        y_peer[1],
        y_peer[2],
        y_peer[3],
        z_peer[1],
        z_peer[2],
        z_peer[6],
        z_peer[7],
        sibling,
        (ahead, dom, core),
        (behind, dom, core),
        (seg, dom_next, core),
        (seg, dom_prev, core),
    ]
    for peer in peers:
        pl.semaphore_signal(barrier, inc=1, device_id=peer, device_id_type=MESH)

    def local_copy(source, target, index):
        return pltpu.make_async_copy(source, target, sem_local.at[index])

    def span(sample):
        return pl.ds(sample * ROWS, ROWS)

    loads = [
        local_copy(w1e_hbm.at[0], w1e, 0),
        local_copy(w2e_hbm.at[0], w2e, 1),
        local_copy(w1n_hbm.at[0], w1n, 2),
        local_copy(w2n_hbm.at[0], w2n, 3),
    ]
    lists = [
        local_copy(send_rows_hbm, send_rows, 20),
        local_copy(sender_row_hbm, sender_row, 21),
        local_copy(receiver_row_hbm, receiver_row, 22),
        local_copy(vectors_hbm.at[0], vectors, 23),
    ]
    starts = []
    finals = []
    for sample in range(SAMPLES):
        starts.append(
            local_copy(node_in.at[sample], table.at[pl.ds(sample * 256, ROWS)], 4 + sample)
        )
        starts.append(local_copy(edge_in.at[sample], edge_x.at[span(sample)], 6 + sample))
        finals.append(local_copy(node_cot.at[sample], d_node.at[span(sample)], 8 + sample))
        finals.append(local_copy(edge_cot.at[sample], d_edge.at[span(sample)], 10 + sample))

    for copy in lists:
        copy.start()

    @pl.when(first)
    def _():
        for copy in starts:
            copy.start()

    for copy in loads:
        copy.start()

    @pl.when(last)
    def _():
        for copy in finals:
            copy.start()

    for copy in lists:
        copy.wait()
    slots = lax.broadcasted_iota(jnp.int32, (2 * ROWS, ROWS), 0)
    own = slots[:ROWS]
    send_t = (own == send_rows[...]).astype(F32)
    recv_t = (own == receiver_row[...]).astype(F32)
    pick_t = (slots == sender_row[...]).astype(F32)
    send_pick = send_t.T.astype(BF16)
    recv_pick = recv_t.T.astype(BF16)
    sender_pick = pick_t.T.astype(BF16)
    send_t = send_t.astype(BF16)
    recv_t = recv_t.astype(BF16)
    pick_t = pick_t.astype(BF16)
    live = (lax.broadcasted_iota(jnp.int32, (ROWS, 1), 0) < edge_count[0]).astype(F32)
    coeffs[...] = vectors[...].astype(F32)

    def coeff(row):
        return coeffs[row : row + 1, :]

    def remote(source, target, sems, index, peer):
        return pltpu.make_async_remote_copy(
            src_ref=source,
            dst_ref=target,
            send_sem=sems.at[0, index],
            recv_sem=sems.at[1, index],
            device_id=peer,
            device_id_type=MESH,
        )

    def halo_copies(source, sample, target_ref, base, kind):
        return (
            remote(
                source.at[pl.ds(sample * ROWS, HALO)],
                target_ref.at[pl.ds(base + HALO, HALO)],
                sem_halo,
                kind * 4 + sample * 2,
                (seg, dom_prev, core),
            ),
            remote(
                source.at[pl.ds(sample * ROWS + HALO, HALO)],
                target_ref.at[pl.ds(base, HALO)],
                sem_halo,
                kind * 4 + sample * 2 + 1,
                (seg, dom_next, core),
            ),
        )

    def out_halo(sample):
        return halo_copies(send_buf, sample, table, sample * 256 + ROWS, 0)

    def back_halo(sample):
        return halo_copies(halo_back, sample, ret, sample * ROWS, 1)

    def node_relay(sample):
        return remote(
            node_o.at[span(sample)],
            table.at[pl.ds(sample * 256, ROWS)],
            sem_relay,
            sample,
            (ahead, dom, core),
        )

    def edge_relay(sample):
        return remote(
            edge_o.at[span(sample)],
            edge_x.at[span(sample)],
            sem_relay,
            2 + sample,
            (ahead, dom, core),
        )

    def node_return(sample):
        return remote(
            d_node_h.at[span(sample)],
            d_node.at[span(sample)],
            sem_relay,
            4 + sample,
            (behind, dom, core),
        )

    def edge_return(sample):
        return remote(
            d_edge_h.at[span(sample)],
            d_edge.at[span(sample)],
            sem_relay,
            6 + sample,
            (behind, dom, core),
        )

    def outputs(sample):
        return (
            local_copy(node_o.at[span(sample)], node_out.at[0, sample], 12 + sample),
            local_copy(edge_o.at[span(sample)], edge_out.at[0, sample], 14 + sample),
        )

    def grad_outputs(sample):
        return (
            local_copy(d_node_f.at[span(sample)], node_grad.at[0, sample], 16 + sample),
            local_copy(d_edge_f.at[span(sample)], edge_grad.at[0, sample], 18 + sample),
        )

    pl.semaphore_wait(barrier, len(peers))

    def lanes_of(side):
        return pl.ds(pl.multiple_of(side * (D // 2), D // 2), D // 2)

    own_feats = local_copy(
        feats.at[:, :, lanes_of(core)], feats_half.at[:, pl.ds(0, SAMPLES * ROWS)], 24
    )
    pair_feats = remote(
        feats.at[:, :, lanes_of(1 - core)],
        feats_half.at[:, pl.ds(SAMPLES * ROWS, SAMPLES * ROWS)],
        sem_pair,
        0,
        sibling,
    )
    pair_vec = remote(vec_acc, vec_sib, sem_pair, 2, sibling)

    def pair_cots(sample, part):
        return remote(
            cot_all.at[pl.ds(2 * part, 2), :, pl.ds(sample * ROWS, ROWS)],
            cot_all.at[pl.ds(2 * part, 2), :, pl.ds((SAMPLES + sample) * ROWS, ROWS)],
            sem_pair,
            3 + 2 * sample + part,
            sibling,
        )

    def either(at_last, when_last, when_not):
        if at_last is None:
            pl.when(last)(when_last)
            pl.when(jnp.logical_not(last))(when_not)
        elif at_last:
            when_last()
        else:
            when_not()

    def backward_main(sample, at_last):
        rows = span(sample)

        either(
            at_last,
            lambda: finals[2 * sample].wait(),
            lambda: node_return(sample).wait_recv(),
        )

        node_back = d_node[rows, :].astype(F32)
        node_norm = norm_n[rows, :]
        node_lin_back = norm_back(node_back * coeff(6), node_norm, scale_n[rows, 0:1])
        lin_half = node_lin_back.astype(BF16)
        node_lin_half = lin_half
        node_pre_back = dot_nt(lin_half, w2n[...]).astype(BF16).astype(F32) * slope_n[rows, :]
        pre_half = node_pre_back.astype(BF16)
        cot_pn[rows, :] = pre_half
        node_pre_half = pre_half
        incoming_back = dot_nt(pre_half, w1n[D:, :]).astype(BF16)
        for index, value in enumerate((node_pre_half, node_lin_half)):
            cot_all[2 + index, :, sample * ROWS : (sample + 1) * ROWS] = value.T
        pair_cots(sample, 1).start()

        either(
            at_last,
            lambda: finals[2 * sample + 1].wait(),
            lambda: edge_return(sample).wait_recv(),
        )

        edge_back = d_edge[rows, :].astype(F32)
        edge_norm = norm_e[rows, :]
        message_back = (edge_back + dot_nn(recv_pick, incoming_back)) * live
        edge_lin_back = norm_back(message_back * coeff(2), edge_norm, scale_e[rows, 0:1])
        lin_half = edge_lin_back.astype(BF16)
        edge_lin_half = lin_half
        edge_pre_back = dot_nt(lin_half, w2e[...]).astype(BF16).astype(F32) * slope_e[rows, :]
        pre_half = edge_pre_back.astype(BF16)
        cot_pe[rows, :] = pre_half
        sender_back = dot_nt(pre_half, w1e[D : 2 * D, :]).astype(BF16)
        halo_back[rows, :] = dot_nn(pick_t[ROWS:, :], sender_back).astype(BF16)
        for copy in back_halo(sample):
            copy.start()
        sender_cot[rows, :] = sender_back
        for index, value in enumerate((pre_half, edge_lin_half)):
            cot_all[index, :, sample * ROWS : (sample + 1) * ROWS] = value.T
        pair_cots(sample, 0).start()
        sums = (
            edge_pre_back,
            edge_lin_back,
            message_back * edge_norm,
            message_back,
            node_pre_back,
            node_lin_back,
            node_back * node_norm,
            node_back,
        )
        for index, value in enumerate(sums):
            vec_acc[sample, index : index + 1, :] = column_sum(value)
        if sample == 1:
            pair_vec.start()
        edge_total = edge_back + dot_nt(pre_half, w1e[:D, :]).astype(BF16).astype(F32)
        d_edge_f[rows, :] = edge_total
        d_edge_h[rows, :] = edge_total.astype(BF16)

        @pl.when(jnp.logical_not(first))
        def _():
            edge_return(sample).start()

    def backward_rest(sample):
        rows = span(sample)
        node_total = d_node[rows, :].astype(F32)
        node_total = node_total + dot_nt(cot_pn[rows, :], w1n[:D, :]).astype(BF16).astype(F32)
        receiver_back = dot_nt(cot_pe[rows, :], w1e[2 * D :, :]).astype(BF16)
        node_total = node_total + dot_nn(pick_t[:ROWS, :], sender_cot[rows, :]).astype(
            BF16
        ).astype(F32)
        node_total = node_total + dot_nn(recv_t, receiver_back).astype(BF16).astype(F32)
        d_node_f[rows, :] = node_total

    def finish(sample):
        rows = span(sample)
        for copy in back_halo(sample):
            copy.wait_recv()
        node_total = d_node_f[rows, :] + dot_nn(send_t, ret[rows, :])
        d_node_f[rows, :] = node_total
        d_node_h[rows, :] = node_total.astype(BF16)

        @pl.when(jnp.logical_not(first))
        def _():
            node_return(sample).start()

        for copy in grad_outputs(sample):
            copy.start()

    def gather(sample):
        nodes = table[pl.ds(sample * 256, ROWS), :]
        send_buf[span(sample), :] = dot_nn(send_pick, nodes).astype(BF16)
        for copy in out_halo(sample):
            copy.start()
        node_x[span(sample), :] = nodes

    @pl.when(first)
    def _():
        for sample in range(SAMPLES):
            starts[2 * sample].wait()
            gather(sample)

    for sample in range(SAMPLES):
        rows = span(sample)
        if sample == 0:

            @pl.when(jnp.logical_not(first))
            def _():
                node_relay(0).wait_recv()
                gather(0)

            for copy in loads:
                copy.wait()
        nodes = node_x[rows, :]
        receivers = dot_nn(recv_pick, nodes).astype(BF16)
        rcv[rows, :] = receivers
        node_part = dot_nn(nodes, w1n[:D, :]) + coeff(4)
        edge_part = dot_nn(receivers, w1e[2 * D :, :]) + coeff(0)

        @pl.when(first)
        def _():
            starts[2 * sample + 1].wait()

        @pl.when(jnp.logical_not(first))
        def _():
            edge_relay(sample).wait_recv()

        edges = edge_x[rows, :]
        edge_part = edge_part + dot_nn(edges, w1e[:D, :])
        if sample == 0:

            @pl.when(jnp.logical_not(first))
            def _():
                node_relay(1).wait_recv()
                gather(1)

        for copy in out_halo(sample):
            copy.wait_recv()
        senders = dot_nn(sender_pick, table[pl.ds(sample * 256, 256), :]).astype(BF16)
        snd[rows, :] = senders
        edge_pre = edge_part + dot_nn(senders, w1e[D : 2 * D, :])
        edge_gate = sigmoid(edge_pre)
        edge_hid = (edge_pre * edge_gate).astype(BF16)
        hid_e[rows, :] = edge_hid
        edge_norm, edge_scale = norm_parts(dot_nn(edge_hid, w2e[...]) + coeff(1))
        norm_e[rows, :] = edge_norm
        scale_e[rows, :] = jnp.broadcast_to(edge_scale, (ROWS, 128))
        message = (edge_norm * coeff(2) + coeff(3)) * live
        edge_o[rows, :] = (edges.astype(F32) + message).astype(BF16)
        if sample == 0:

            @pl.when(jnp.logical_not(last))
            def _():
                edge_relay(0).start()

        incoming = dot_nn(recv_t, message.astype(BF16)).astype(BF16)
        inc[rows, :] = incoming
        node_pre = node_part + dot_nn(incoming, w1n[D:, :])
        node_gate = sigmoid(node_pre)
        node_hid = (node_pre * node_gate).astype(BF16)
        hid_n[rows, :] = node_hid
        node_norm, node_scale = norm_parts(dot_nn(node_hid, w2n[...]) + coeff(5))
        norm_n[rows, :] = node_norm
        scale_n[rows, :] = jnp.broadcast_to(node_scale, (ROWS, 128))
        node_o[rows, :] = (nodes.astype(F32) + node_norm * coeff(6) + coeff(7)).astype(BF16)

        @pl.when(jnp.logical_not(last))
        def _():
            node_relay(sample).start()

        for copy in outputs(sample):
            copy.start()
        slope_e[rows, :] = edge_gate * (1.0 + edge_pre * (1.0 - edge_gate))
        slope_n[rows, :] = node_gate * (1.0 + node_pre * (1.0 - node_gate))
        if sample == 0:

            @pl.when(last)
            def _():
                backward_main(0, True)
                backward_rest(0)

    @pl.when(jnp.logical_not(last))
    def _():
        node_relay(1).wait_send()
        edge_relay(1).start()

    own_feats.start()
    pair_feats.start()

    @pl.when(jnp.logical_not(last))
    def _():
        backward_main(0, False)
        backward_rest(0)

    finish(0)
    backward_main(1, None)

    def wide(ref):
        return ref[...].astype(F32)

    class YFold:
        def __init__(self, source, load, cut, parts, base):
            fold_p, fold_m, self.stage_p, self.stage_m, self.p0, self.p1, self.m0, self.m1 = parts
            low, high = slice(0, cut), slice(cut, None)
            self.load, self.low, self.high = load, low, high
            self.fold_p, self.fold_m = fold_p, fold_m

            def send(src, target, index, peer):
                return remote(src, target, sem_y, base + index, y_peer[peer])

            self.fp = send(source(y_at[2], low), fold_p, 0, 1)
            self.fm = send(source(y_at[2], high), fold_m, 1, 3)
            self.c_p1 = send(source(y_at[1], high), self.p1, 2, 1)
            self.c_m0 = send(source(y_at[3], low), self.m0, 3, 3)
            self.c_p0 = send(self.stage_p, self.p0, 4, 1)
            self.c_m1 = send(self.stage_m, self.m1, 5, 3)
            self.all = (self.fp, self.fm, self.c_p1, self.c_m0, self.c_p0, self.c_m1)

        def start(self):
            for copy in self.all[:4]:
                copy.start()

        def middle(self):
            self.fp.wait_recv()
            total = self.load(y_at[1], self.low).astype(F32) + wide(self.fold_p)
            self.stage_p[...] = total.astype(BF16)
            self.c_p0.start()
            self.fm.wait_recv()
            total = self.load(y_at[3], self.high).astype(F32) + wide(self.fold_m)
            self.stage_m[...] = total.astype(BF16)
            self.c_m1.start()

        def finish(self):
            for copy in self.all[2:]:
                copy.wait_recv()
            low = self.load(y_at[0], self.low).astype(F32) + wide(self.p0) + wide(self.m0)
            high = self.load(y_at[0], self.high).astype(F32) + wide(self.p1) + wide(self.m1)
            return low, high

    class ZFold:
        def __init__(self, source, cut, parts, base):
            self.r4p, self.r4m, self.r3p, self.r3m, self.r1p, self.r1m = parts[:6]
            self.stage_p, self.stage_m, self.r2p, self.r2m = parts[6:]
            self.source, self.cut = source, cut

            def send(src, target, index, peer):
                return remote(src, target, sem_z, base + index, z_peer[peer])

            far = source.at[z_at[4]]
            self.all = (
                send(far.at[..., :cut], self.r4p, 0, 2),
                send(far.at[..., cut:], self.r4m, 1, 6),
                send(source.at[z_at[3]], self.r3p, 2, 1),
                send(source.at[z_at[5]], self.r3m, 3, 7),
                send(source.at[z_at[1]], self.r1p, 4, 1),
                send(source.at[z_at[7]], self.r1m, 5, 7),
                send(self.stage_p, self.r2p, 6, 2),
                send(self.stage_m, self.r2m, 7, 6),
            )

        def start(self):
            for copy in self.all[:6]:
                copy.start()

        def middle(self):
            cut = self.cut
            self.all[2].wait_recv()
            self.all[0].wait_recv()
            total = self.source[z_at[2]].astype(F32) + wide(self.r3p)
            self.stage_p[..., cut:] = total[..., cut:].astype(BF16)
            self.stage_p[..., :cut] = (total[..., :cut] + wide(self.r4p)).astype(BF16)
            self.all[6].start()
            self.all[3].wait_recv()
            self.all[1].wait_recv()
            total = self.source[z_at[6]].astype(F32) + wide(self.r3m)
            self.stage_m[..., :cut] = total[..., :cut].astype(BF16)
            self.stage_m[..., cut:] = (total[..., cut:] + wide(self.r4m)).astype(BF16)
            self.all[7].start()

        def finish(self):
            for copy in self.all[4:]:
                copy.wait_recv()
            total = self.source[z_at[0]].astype(F32) + wide(self.r1p) + wide(self.r1m)
            return total + wide(self.r2p) + wide(self.r2m)

    def folds(source, half, y_bufs, z_bufs, cut, y_base, z_base):
        y_fold = YFold(
            lambda at, lanes: source.at[:, at, :, lanes],
            lambda at, lanes: source[:, at, :, lanes],
            cut,
            y_bufs,
            y_base,
        )
        return y_fold, ZFold(half, cut, z_bufs, z_base)

    a_y, a_z = folds(sum_a, half_a, fold_ay, fold_az, CUT_A, 0, 8)
    v_y, v_z = folds(sum_v, half_v, fold_vy, fold_vz, CUT_V, 6, 16)
    b_z = ZFold(sum_b, CUT_B, fold_bz, 0)
    b_y = [
        remote(half_b.at[y_at[k]], recv_by.at[k - 1], sem_y, 11 + k, y_peer[k])
        for k in range(1, NY)
    ]

    own_feats.wait()
    pair_feats.wait_recv()
    for sample in range(SAMPLES):
        pair_cots(sample, 1).wait_recv()

    def spread(value):
        return value.astype(BF16).reshape(NZ, NY, 16, value.shape[1])

    width = D // 2
    for index, which in enumerate((2, 2, 3)):
        value = dot_nn(cot_all[which], feats_half[4 + index])
        sum_b[:, :, :, index * width : (index + 1) * width] = spread(value)
    pl.when(first)(b_z.start)
    for sample in range(SAMPLES):
        pair_cots(sample, 0).wait_recv()
    for index in range(2):
        value = dot_nn(cot_all[0], feats_half[index])
        sum_a[:, :, :, index * width : (index + 1) * width] = spread(value)
    pl.when(first)(a_y.start)
    for index, which in enumerate((0, 1)):
        value = dot_nn(cot_all[which], feats_half[2 + index])
        sum_v[:, :, :, index * width : (index + 1) * width] = spread(value)
    pair_vec.wait_recv()
    vec_sum = vec_acc[0] + vec_acc[1] + vec_sib[0] + vec_sib[1]
    vec_block = jnp.concatenate([vec_sum, jnp.zeros((120, D), F32)], 0).T
    sum_v[:, :, :, 2 * width :] = spread(vec_block)
    pl.when(first)(v_y.start)
    backward_rest(1)
    finish(1)

    @pl.when(jnp.logical_not(first))
    def _():
        b_z.start()
        a_y.start()
        v_y.start()

    def joined(parts):
        return jnp.concatenate(parts, -1)

    def keep(value, start):
        lanes = slice(start, start + value.shape[1])
        fin[0, :, lanes] = value[:8]
        fin[1, :, lanes] = value[8:]

    a_y.middle()
    b_z.middle()
    v_y.middle()
    half_a[...] = joined(a_y.finish()).astype(BF16)
    a_z.start()
    half_v[...] = joined(v_y.finish()).astype(BF16)
    v_z.start()
    half_b[...] = b_z.finish().astype(BF16)
    for copy in b_y:
        copy.start()
    a_z.middle()
    v_z.middle()
    total = half_b[y_at[0]].astype(F32)
    for index, copy in enumerate(b_y):
        copy.wait_recv()
        total = total + recv_by[index].astype(F32)
    keep(total, LANES_A + LANES_V)
    keep(a_z.finish(), 0)
    keep(v_z.finish(), LANES_A)
    swap = remote(fin.at[1 - core], fin_sib, sem_pair, 1, sibling)
    swap.start()
    swap.wait_recv()
    grads_out[core] = fin[core]
    grads_out[1 - core] = fin_sib[...]

    swap.wait_send()
    pair_feats.wait_send()
    pair_vec.wait_send()
    for sample in range(SAMPLES):
        pair_cots(sample, 0).wait_send()
        pair_cots(sample, 1).wait_send()
    for copy in (*a_y.all, *b_z.all, *a_z.all, *v_y.all, *v_z.all, *b_y):
        copy.wait_send()
    for sample in range(SAMPLES):
        for copy in out_halo(sample) + back_halo(sample):
            copy.wait_send()
        for copy in outputs(sample) + grad_outputs(sample):
            copy.wait()

        @pl.when(jnp.logical_not(last))
        def _():
            edge_relay(sample).wait_send()
            if sample == 0:
                node_relay(0).wait_send()

        @pl.when(jnp.logical_not(first))
        def _():
            edge_return(sample).wait_send()
            node_return(sample).wait_send()


def store_kernel(node_out, edge_out, node_grad, edge_grad, grads_hbm, *refs):
    results, held, rows_held, grads, sems = refs[:9], refs[9:13], refs[13:18], refs[18], refs[19]
    grads_load = pltpu.make_async_copy(grads_hbm, grads, sems.at[13])
    grads_load.start()
    sources = (node_out, edge_out, node_grad, edge_grad)
    loads = [
        pltpu.make_async_copy(source, target, sems.at[index])
        for index, (source, target) in enumerate(zip(sources, held))
    ]
    stores = [
        pltpu.make_async_copy(source, target, sems.at[4 + index])
        for index, (source, target) in enumerate(zip(held + rows_held, results))
    ]
    for copy in loads:
        copy.start()
    w1e_rows, w2e_rows, w1n_rows, w2n_rows, vec_rows = rows_held
    grads_load.wait()
    width = D // 2
    places = [(w1e_rows, 0), (w1e_rows, D), (w1e_rows, 2 * D), (w2e_rows, 0)]
    places += [(w1n_rows, 0), (w1n_rows, D), (w2n_rows, 0)]
    for index, (target, start) in enumerate(places):
        lane = index * width if index < 4 else HALF - LANES_B + (index - 4) * width
        for side in range(2):
            target[:, start + side * width : start + (side + 1) * width] = grads[
                side, :, lane : lane + width
            ]
    columns = grads[0, :, 4 * width : 4 * width + 128].T
    vec_rows[...] = columns[:8, :]
    for copy in stores[4:]:
        copy.start()
    for load, copy in zip(loads, stores):
        load.wait()
        copy.start()
    for copy in stores:
        copy.wait()


def local(
    node_in,
    edge_in,
    node_cot,
    edge_cot,
    send_rows,
    sender_row,
    receiver_row,
    edge_count,
    edge_w1,
    edge_w2,
    node_w1,
    node_w2,
    vectors,
):
    anywhere = pl.BlockSpec(memory_space=pl.ANY)
    vmem = pl.BlockSpec(memory_space=pltpu.VMEM)
    smem = pl.BlockSpec(memory_space=pltpu.SMEM)
    both = SAMPLES * ROWS

    def half(*shape):
        return pltpu.VMEM(shape, BF16)

    def full(*shape):
        return pltpu.VMEM(shape, F32)

    def y_parts(lead, lanes, cut):
        low, high = half(*lead, cut), half(*lead, lanes - cut)
        return [low, high, low, high, low, high, low, high]

    def z_parts(lead, lanes, cut):
        return [half(*lead, cut), half(*lead, lanes - cut)] + [half(*lead, lanes)] * 8

    scratch = [
        half(3 * D, D),
        half(D, D),
        half(2 * D, D),
        half(D, D),
        pltpu.VMEM((1, ROWS), jnp.int32),
        pltpu.VMEM((1, ROWS), jnp.int32),
        pltpu.VMEM((1, ROWS), jnp.int32),
        half(8, D),
        full(8, D),
        half(2 * both, D),
        half(7, both, D),
        half(7, 2 * both, D // 2),
        full(both, D),
        full(both, D),
        full(both, 128),
        full(both, D),
        full(both, D),
        full(both, 128),
        half(both, D),
        half(both, D),
        half(both, D),
        half(both, D),
        half(both, D),
        full(both, D),
        full(both, D),
        half(both, D),
        half(both, D),
        half(both, D),
        half(both, D),
        half(both, D),
        half(both, D),
        half(both, D),
        half(4, D, 2 * both),
        full(SAMPLES, 8, D),
        full(SAMPLES, 8, D),
        half(NZ, NY, 16, LANES_A),
        half(NZ, NY, 16, LANES_V),
        half(NZ, NY, 16, LANES_B),
        half(NZ, 16, LANES_A),
        half(NZ, 16, LANES_V),
        half(NY, 16, LANES_B),
        y_parts((NZ, 16), LANES_A, CUT_A),
        y_parts((NZ, 16), LANES_V, CUT_V),
        z_parts((NY, 16), LANES_B, CUT_B),
        z_parts((16,), LANES_A, CUT_A),
        z_parts((16,), LANES_V, CUT_V),
        half(NY - 1, 16, LANES_B),
        full(2, 8, HALF),
        full(8, HALF),
        pltpu.SemaphoreType.DMA((25,)),
        pltpu.SemaphoreType.DMA((2, 8)),
        pltpu.SemaphoreType.DMA((2, 8)),
        pltpu.SemaphoreType.DMA((2, 7)),
        pltpu.SemaphoreType.DMA((2, 15)),
        pltpu.SemaphoreType.DMA((2, 24)),
    ]
    shape = (1, SAMPLES, ROWS, D)
    node_out, edge_out, node_grad, edge_grad, grads = pl.pallas_call(
        kernel,
        out_shape=(
            jax.ShapeDtypeStruct(shape, BF16),
            jax.ShapeDtypeStruct(shape, BF16),
            jax.ShapeDtypeStruct(shape, F32),
            jax.ShapeDtypeStruct(shape, F32),
            jax.ShapeDtypeStruct((2, 8, HALF), F32),
        ),
        in_specs=[anywhere] * 7 + [smem] + [anywhere] * 5,
        out_specs=(anywhere,) * 4 + (vmem,),
        scratch_shapes=scratch,
        compiler_params=pltpu.CompilerParams(
            collective_id=0, has_side_effects=True, vmem_limit_bytes=60 << 20
        ),
        name="layers",
    )(
        node_in,
        edge_in,
        node_cot,
        edge_cot,
        send_rows.reshape(1, ROWS),
        sender_row.reshape(1, ROWS),
        receiver_row.reshape(1, ROWS),
        edge_count,
        edge_w1,
        edge_w2,
        node_w1,
        node_w2,
        vectors,
    )
    rows_of = (3 * D, D, 2 * D, D, 8)
    results = pl.pallas_call(
        store_kernel,
        out_shape=(
            jax.ShapeDtypeStruct(shape, BF16),
            jax.ShapeDtypeStruct(shape, BF16),
            jax.ShapeDtypeStruct(shape, F32),
            jax.ShapeDtypeStruct(shape, F32),
        )
        + tuple(jax.ShapeDtypeStruct((8, rows), F32) for rows in rows_of),
        in_specs=[anywhere] * 5,
        out_specs=(anywhere,) * 9,
        scratch_shapes=[pltpu.VMEM(shape, BF16)] * 2
        + [pltpu.VMEM(shape, F32)] * 2
        + [pltpu.VMEM((8, rows), F32) for rows in rows_of]
        + [pltpu.VMEM((2, 8, HALF), F32), pltpu.SemaphoreType.DMA((14,))],
        name="store",
    )(node_out, edge_out, node_grad, edge_grad, grads)
    return results[:4] + tuple(value.T[None] for value in results[4:8]) + (results[8][None],)


def solution(mesh):
    in_specs = (
        P("dp", "dom", None),
        P("dp", "dom", None),
        P("dp", "dom", None),
        P("dp", "dom", None),
        P("dom"),
        P("dom"),
        P("dom"),
        P("dom"),
        P("segment", None, None),
        P("segment", None, None),
        P("segment", None, None),
        P("segment", None, None),
        P("segment", None, None),
    )
    out_specs = (
        P("segment", "dp", "dom", None),
        P("segment", "dp", "dom", None),
        P("segment", "dp", "dom", None),
        P("segment", "dp", "dom", None),
        P("segment", None, ("dom", "dp")),
        P("segment", None, ("dom", "dp")),
        P("segment", None, ("dom", "dp")),
        P("segment", None, ("dom", "dp")),
        P("segment", None, ("dom", "dp")),
    )
    return jax.shard_map(local, mesh=mesh, in_specs=in_specs, out_specs=out_specs, check_vma=False)
```

```python
import functools

import jax
import jax.numpy as jnp
from jax import lax
from jax.experimental import pallas as pl
from jax.experimental.pallas import tpu as pltpu
from jax.sharding import PartitionSpec as P

F32 = jnp.float32
BF16 = jnp.bfloat16
MESH = pl.DeviceIdType.MESH

D = 512
ROWS = 128
HALO = 64
SAMPLES = 2
NY = 4
NZ = 8
DOMS = NY * NZ
SECTIONS = 4
HALF = 1920
LANES_A = 512
LANES_V = 640
LANES_B = HALF - LANES_A - LANES_V
CUT_A = 256
CUT_V = 384
CUT_B = 384


def dot_nn(left, right):
    return jnp.dot(left, right, preferred_element_type=F32)


def dot_nt(left, right):
    return lax.dot_general(left, right, (((1,), (1,)), ((), ())), preferred_element_type=F32)


def sigmoid(values):
    return 0.5 * jnp.tanh(0.5 * values) + 0.5


def norm_parts(values):
    average = jnp.mean(values, -1, keepdims=True)
    centred = values - average
    scale = lax.rsqrt(jnp.mean(centred * centred, -1, keepdims=True) + 1e-05)
    return centred * scale, scale


def norm_back(cotangent, normed, scale):
    first = jnp.mean(cotangent, -1, keepdims=True)
    second = jnp.mean(cotangent * normed, -1, keepdims=True)
    return scale * (cotangent - first - normed * second)


def column_sum(values):
    return jnp.sum(values, 0, keepdims=True)


def kernel(
    node_in,
    edge_in,
    node_cot,
    edge_cot,
    send_rows_hbm,
    sender_row_hbm,
    receiver_row_hbm,
    edge_count,
    w1e_hbm,
    w2e_hbm,
    w1n_hbm,
    w2n_hbm,
    vectors_hbm,
    node_out,
    edge_out,
    node_grad,
    edge_grad,
    grads_out,
    w1e,
    w2e,
    w1n,
    w2n,
    send_rows,
    sender_row,
    receiver_row,
    vectors,
    coeffs,
    table,
    feats,
    feats_half,
    slope_e,
    norm_e,
    scale_e,
    slope_n,
    norm_n,
    scale_n,
    node_o,
    edge_o,
    send_buf,
    d_node,
    d_edge,
    d_node_f,
    d_edge_f,
    d_node_h,
    d_edge_h,
    halo_back,
    ret,
    cot_pe,
    cot_pn,
    sender_cot,
    cot_all,
    vec_acc,
    vec_sib,
    sum_a,
    sum_v,
    sum_b,
    half_a,
    half_v,
    half_b,
    fold_ay,
    fold_vy,
    fold_bz,
    fold_az,
    fold_vz,
    recv_by,
    fin,
    fin_sib,
    sem_local,
    sem_relay,
    sem_halo,
    sem_pair,
    sem_y,
    sem_z,
):
    seg = lax.axis_index("segment")
    dom = lax.axis_index("dom")
    core = lax.axis_index("dp")
    zed = dom // NY
    why = dom % NY
    first = seg == 0
    last = seg == SECTIONS - 1
    ahead = lax.rem(seg + 1, SECTIONS)
    behind = lax.rem(seg + SECTIONS - 1, SECTIONS)
    dom_next = lax.rem(dom + 1, DOMS)
    dom_prev = lax.rem(dom + DOMS - 1, DOMS)
    y_at = [lax.rem(why + k, NY) for k in range(NY)]
    z_at = [lax.rem(zed + k, NZ) for k in range(NZ)]
    y_peer = [(seg, zed * NY + at, core) for at in y_at]
    z_peer = [(seg, at * NY + why, core) for at in z_at]
    sibling = (seg, dom, 1 - core)

    edge_x, snd, rcv, hid_e, node_x, inc, hid_n = [feats.at[index] for index in range(7)]

    barrier = pltpu.get_barrier_semaphore()
    peers = [
        y_peer[1],
        y_peer[2],
        y_peer[3],
        z_peer[1],
        z_peer[2],
        z_peer[6],
        z_peer[7],
        sibling,
        (ahead, dom, core),
        (behind, dom, core),
        (seg, dom_next, core),
        (seg, dom_prev, core),
    ]
    for peer in peers:
        pl.semaphore_signal(barrier, inc=1, device_id=peer, device_id_type=MESH)

    def local_copy(source, target, index):
        return pltpu.make_async_copy(source, target, sem_local.at[index])

    def span(sample):
        return pl.ds(sample * ROWS, ROWS)

    loads = [
        local_copy(w1e_hbm.at[0], w1e, 0),
        local_copy(w2e_hbm.at[0], w2e, 1),
        local_copy(w1n_hbm.at[0], w1n, 2),
        local_copy(w2n_hbm.at[0], w2n, 3),
    ]
    lists = [
        local_copy(send_rows_hbm, send_rows, 20),
        local_copy(sender_row_hbm, sender_row, 21),
        local_copy(receiver_row_hbm, receiver_row, 22),
        local_copy(vectors_hbm.at[0], vectors, 23),
    ]
    starts = []
    finals = []
    for sample in range(SAMPLES):
        starts.append(
            local_copy(node_in.at[sample], table.at[pl.ds(sample * 256, ROWS)], 4 + sample)
        )
        starts.append(local_copy(edge_in.at[sample], edge_x.at[span(sample)], 6 + sample))
        finals.append(local_copy(node_cot.at[sample], d_node.at[span(sample)], 8 + sample))
        finals.append(local_copy(edge_cot.at[sample], d_edge.at[span(sample)], 10 + sample))

    for copy in lists:
        copy.start()

    @pl.when(first)
    def _():
        for copy in starts:
            copy.start()

    for copy in loads:
        copy.start()

    @pl.when(last)
    def _():
        for copy in finals:
            copy.start()

    for copy in lists:
        copy.wait()
    slots = lax.broadcasted_iota(jnp.int32, (2 * ROWS, ROWS), 0)
    own = slots[:ROWS]
    send_t = (own == send_rows[...]).astype(F32)
    recv_t = (own == receiver_row[...]).astype(F32)
    pick_t = (slots == sender_row[...]).astype(F32)
    send_pick = send_t.T.astype(BF16)
    recv_pick = recv_t.T.astype(BF16)
    sender_pick = pick_t.T.astype(BF16)
    send_t = send_t.astype(BF16)
    recv_t = recv_t.astype(BF16)
    pick_t = pick_t.astype(BF16)
    live = (lax.broadcasted_iota(jnp.int32, (ROWS, 1), 0) < edge_count[0]).astype(F32)
    coeffs[...] = vectors[...].astype(F32)

    def coeff(row):
        return coeffs[row : row + 1, :]

    def remote(source, target, sems, index, peer):
        return pltpu.make_async_remote_copy(
            src_ref=source,
            dst_ref=target,
            send_sem=sems.at[0, index],
            recv_sem=sems.at[1, index],
            device_id=peer,
            device_id_type=MESH,
        )

    def part_of(part):
        return pl.ds(part * (D // 2), D // 2)

    def halo_copies(source, sample, part, target_ref, base, kind):
        index = kind * 8 + sample * 4 + part * 2
        lanes = part_of(part)
        return (
            remote(
                source.at[pl.ds(sample * ROWS, HALO), lanes],
                target_ref.at[pl.ds(base + HALO, HALO), lanes],
                sem_halo,
                index,
                (seg, dom_prev, core),
            ),
            remote(
                source.at[pl.ds(sample * ROWS + HALO, HALO), lanes],
                target_ref.at[pl.ds(base, HALO), lanes],
                sem_halo,
                index + 1,
                (seg, dom_next, core),
            ),
        )

    def out_halo(sample, part):
        return halo_copies(send_buf, sample, part, table, sample * 256 + ROWS, 0)

    def back_halo(sample, part):
        return halo_copies(halo_back, sample, part, ret, sample * ROWS, 1)

    def node_relay(sample, part):
        return remote(
            node_o.at[span(sample), part_of(part)],
            table.at[pl.ds(sample * 256, ROWS), part_of(part)],
            sem_relay,
            sample * 2 + part,
            (ahead, dom, core),
        )

    def edge_relay(sample):
        return remote(
            edge_o.at[span(sample)],
            edge_x.at[span(sample)],
            sem_relay,
            4 + sample,
            (ahead, dom, core),
        )

    def node_return(sample, part):
        return remote(
            d_node_h.at[span(sample), part_of(part)],
            d_node.at[span(sample), part_of(part)],
            sem_relay,
            6 + sample * 2 + part,
            (behind, dom, core),
        )

    def edge_return(sample):
        return remote(
            d_edge_h.at[span(sample)],
            d_edge.at[span(sample)],
            sem_relay,
            10 + sample,
            (behind, dom, core),
        )

    def outputs(sample):
        return (
            local_copy(node_o.at[span(sample)], node_out.at[0, sample], 12 + sample),
            local_copy(edge_o.at[span(sample)], edge_out.at[0, sample], 14 + sample),
        )

    def grad_outputs(sample):
        return (
            local_copy(d_node_f.at[span(sample)], node_grad.at[0, sample], 16 + sample),
            local_copy(d_edge_f.at[span(sample)], edge_grad.at[0, sample], 18 + sample),
        )

    pl.semaphore_wait(barrier, len(peers))

    def lanes_of(side):
        return pl.ds(pl.multiple_of(side * (D // 2), D // 2), D // 2)

    own_feats = local_copy(
        feats.at[:, :, lanes_of(core)], feats_half.at[:, pl.ds(0, SAMPLES * ROWS)], 24
    )
    pair_feats = remote(
        feats.at[:, :, lanes_of(1 - core)],
        feats_half.at[:, pl.ds(SAMPLES * ROWS, SAMPLES * ROWS)],
        sem_pair,
        0,
        sibling,
    )
    pair_vec = remote(vec_acc, vec_sib, sem_pair, 2, sibling)

    def pair_cots(sample, part):
        return remote(
            cot_all.at[pl.ds(2 * part, 2), :, pl.ds(sample * ROWS, ROWS)],
            cot_all.at[pl.ds(2 * part, 2), :, pl.ds((SAMPLES + sample) * ROWS, ROWS)],
            sem_pair,
            3 + 2 * sample + part,
            sibling,
        )

    def either(at_last, when_last, when_not):
        if at_last is None:
            pl.when(last)(when_last)
            pl.when(jnp.logical_not(last))(when_not)
        elif at_last:
            when_last()
        else:
            when_not()

    def backward_main(sample, at_last):
        rows = span(sample)

        either(
            at_last,
            lambda: finals[2 * sample].wait(),
            lambda: [node_return(sample, part).wait_recv() for part in range(2)] and None,
        )

        node_back = d_node[rows, :].astype(F32)
        node_norm = norm_n[rows, :]
        node_lin_back = norm_back(node_back * coeff(6), node_norm, scale_n[rows, 0:1])
        lin_half = node_lin_back.astype(BF16)
        node_lin_half = lin_half
        node_pre_back = dot_nt(lin_half, w2n[...]).astype(BF16).astype(F32) * slope_n[rows, :]
        pre_half = node_pre_back.astype(BF16)
        cot_pn[rows, :] = pre_half
        node_pre_half = pre_half
        incoming_back = dot_nt(pre_half, w1n[D:, :]).astype(BF16)
        for index, value in enumerate((node_pre_half, node_lin_half)):
            cot_all[2 + index, :, sample * ROWS : (sample + 1) * ROWS] = value.T
        pair_cots(sample, 1).start()

        either(
            at_last,
            lambda: finals[2 * sample + 1].wait(),
            lambda: edge_return(sample).wait_recv(),
        )

        edge_back = d_edge[rows, :].astype(F32)
        edge_norm = norm_e[rows, :]
        message_back = (edge_back + dot_nn(recv_pick, incoming_back)) * live
        edge_lin_back = norm_back(message_back * coeff(2), edge_norm, scale_e[rows, 0:1])
        lin_half = edge_lin_back.astype(BF16)
        edge_lin_half = lin_half
        edge_pre_back = dot_nt(lin_half, w2e[...]).astype(BF16).astype(F32) * slope_e[rows, :]
        pre_half = edge_pre_back.astype(BF16)
        cot_pe[rows, :] = pre_half
        for part in range(2):
            lanes = slice(part * (D // 2), (part + 1) * (D // 2))
            sender_back = dot_nt(
                pre_half, w1e[D + part * (D // 2) : D + (part + 1) * (D // 2), :]
            ).astype(BF16)
            halo_back[rows, lanes] = dot_nn(pick_t[ROWS:, :], sender_back).astype(BF16)
            for copy in back_halo(sample, part):
                copy.start()
            sender_cot[rows, lanes] = sender_back
        for index, value in enumerate((pre_half, edge_lin_half)):
            cot_all[index, :, sample * ROWS : (sample + 1) * ROWS] = value.T
        pair_cots(sample, 0).start()
        sums = (
            edge_pre_back,
            edge_lin_back,
            message_back * edge_norm,
            message_back,
            node_pre_back,
            node_lin_back,
            node_back * node_norm,
            node_back,
        )
        for index, value in enumerate(sums):
            vec_acc[sample, index : index + 1, :] = column_sum(value)
        if sample == 1:
            pair_vec.start()
        edge_total = edge_back + dot_nt(pre_half, w1e[:D, :]).astype(BF16).astype(F32)
        d_edge_f[rows, :] = edge_total
        d_edge_h[rows, :] = edge_total.astype(BF16)

        @pl.when(jnp.logical_not(first))
        def _():
            edge_return(sample).start()

    def backward_rest(sample):
        rows = span(sample)
        node_total = d_node[rows, :].astype(F32)
        node_total = node_total + dot_nt(cot_pn[rows, :], w1n[:D, :]).astype(BF16).astype(F32)
        receiver_back = dot_nt(cot_pe[rows, :], w1e[2 * D :, :]).astype(BF16)
        node_total = node_total + dot_nn(pick_t[:ROWS, :], sender_cot[rows, :]).astype(
            BF16
        ).astype(F32)
        node_total = node_total + dot_nn(recv_t, receiver_back).astype(BF16).astype(F32)
        d_node_f[rows, :] = node_total

    def finish(sample):
        rows = span(sample)
        for part in range(2):
            lanes = slice(part * (D // 2), (part + 1) * (D // 2))
            for copy in back_halo(sample, part):
                copy.wait_recv()
            node_total = d_node_f[rows, lanes] + dot_nn(send_t, ret[rows, lanes])
            d_node_f[rows, lanes] = node_total
            d_node_h[rows, lanes] = node_total.astype(BF16)
            pl.when(jnp.logical_not(first))(node_return(sample, part).start)

        for copy in grad_outputs(sample):
            copy.start()

    def gather(sample, relayed):
        for part in range(2):
            lanes = slice(part * (D // 2), (part + 1) * (D // 2))
            if relayed:
                node_relay(sample, part).wait_recv()
            nodes = table[pl.ds(sample * 256, ROWS), lanes]
            send_buf[span(sample), lanes] = dot_nn(send_pick, nodes).astype(BF16)
            for copy in out_halo(sample, part):
                copy.start()
            node_x[span(sample), lanes] = nodes

    @pl.when(first)
    def _():
        for sample in range(SAMPLES):
            starts[2 * sample].wait()
            gather(sample, False)

    for sample in range(SAMPLES):
        rows = span(sample)
        if sample == 0:

            @pl.when(jnp.logical_not(first))
            def _():
                gather(0, True)

            for copy in loads:
                copy.wait()
        nodes = node_x[rows, :]
        receivers = dot_nn(recv_pick, nodes).astype(BF16)
        rcv[rows, :] = receivers
        node_part = dot_nn(nodes, w1n[:D, :]) + coeff(4)
        edge_part = dot_nn(receivers, w1e[2 * D :, :]) + coeff(0)

        @pl.when(first)
        def _():
            starts[2 * sample + 1].wait()

        @pl.when(jnp.logical_not(first))
        def _():
            edge_relay(sample).wait_recv()

        edges = edge_x[rows, :]
        edge_part = edge_part + dot_nn(edges, w1e[:D, :])
        if sample == 0:

            @pl.when(jnp.logical_not(first))
            def _():
                gather(1, True)

        for part in range(2):
            for copy in out_halo(sample, part):
                copy.wait_recv()
        senders = dot_nn(sender_pick, table[pl.ds(sample * 256, 256), :]).astype(BF16)
        snd[rows, :] = senders
        edge_pre = edge_part + dot_nn(senders, w1e[D : 2 * D, :])
        edge_gate = sigmoid(edge_pre)
        edge_hid = (edge_pre * edge_gate).astype(BF16)
        hid_e[rows, :] = edge_hid
        edge_norm, edge_scale = norm_parts(dot_nn(edge_hid, w2e[...]) + coeff(1))
        norm_e[rows, :] = edge_norm
        scale_e[rows, :] = jnp.broadcast_to(edge_scale, (ROWS, 128))
        message = (edge_norm * coeff(2) + coeff(3)) * live
        edge_o[rows, :] = (edges.astype(F32) + message).astype(BF16)
        if sample == 0:

            @pl.when(jnp.logical_not(last))
            def _():
                edge_relay(0).start()

        incoming = dot_nn(recv_t, message.astype(BF16)).astype(BF16)
        inc[rows, :] = incoming
        node_pre = node_part + dot_nn(incoming, w1n[D:, :])
        node_gate = sigmoid(node_pre)
        node_hid = (node_pre * node_gate).astype(BF16)
        hid_n[rows, :] = node_hid
        node_norm, node_scale = norm_parts(dot_nn(node_hid, w2n[...]) + coeff(5))
        norm_n[rows, :] = node_norm
        scale_n[rows, :] = jnp.broadcast_to(node_scale, (ROWS, 128))
        node_o[rows, :] = (nodes.astype(F32) + node_norm * coeff(6) + coeff(7)).astype(BF16)

        @pl.when(jnp.logical_not(last))
        def _():
            for part in range(2):
                node_relay(sample, part).start()

        for copy in outputs(sample):
            copy.start()
        slope_e[rows, :] = edge_gate * (1.0 + edge_pre * (1.0 - edge_gate))
        slope_n[rows, :] = node_gate * (1.0 + node_pre * (1.0 - node_gate))
        if sample == 0:

            @pl.when(last)
            def _():
                backward_main(0, True)
                backward_rest(0)

    @pl.when(jnp.logical_not(last))
    def _():
        for part in range(2):
            node_relay(1, part).wait_send()
        edge_relay(1).start()

    own_feats.start()
    pair_feats.start()

    @pl.when(jnp.logical_not(last))
    def _():
        backward_main(0, False)
        backward_rest(0)

    finish(0)
    backward_main(1, None)

    def wide(ref):
        return ref[...].astype(F32)

    class YFold:
        def __init__(self, source, load, cut, parts, base):
            fold_p, fold_m, self.stage_p, self.stage_m, self.p0, self.p1, self.m0, self.m1 = parts
            low, high = slice(0, cut), slice(cut, None)
            self.load, self.low, self.high = load, low, high
            self.fold_p, self.fold_m = fold_p, fold_m

            def send(src, target, index, peer):
                return remote(src, target, sem_y, base + index, y_peer[peer])

            self.fp = send(source(y_at[2], low), fold_p, 0, 1)
            self.fm = send(source(y_at[2], high), fold_m, 1, 3)
            self.c_p1 = send(source(y_at[1], high), self.p1, 2, 1)
            self.c_m0 = send(source(y_at[3], low), self.m0, 3, 3)
            self.c_p0 = send(self.stage_p, self.p0, 4, 1)
            self.c_m1 = send(self.stage_m, self.m1, 5, 3)
            self.all = (self.fp, self.fm, self.c_p1, self.c_m0, self.c_p0, self.c_m1)

        def start(self):
            for copy in self.all[:4]:
                copy.start()

        def middle(self):
            self.fp.wait_recv()
            total = self.load(y_at[1], self.low).astype(F32) + wide(self.fold_p)
            self.stage_p[...] = total.astype(BF16)
            self.c_p0.start()
            self.fm.wait_recv()
            total = self.load(y_at[3], self.high).astype(F32) + wide(self.fold_m)
            self.stage_m[...] = total.astype(BF16)
            self.c_m1.start()

        def finish(self):
            for copy in self.all[2:]:
                copy.wait_recv()
            low = self.load(y_at[0], self.low).astype(F32) + wide(self.p0) + wide(self.m0)
            high = self.load(y_at[0], self.high).astype(F32) + wide(self.p1) + wide(self.m1)
            return low, high

    class ZFold:
        def __init__(self, source, cut, parts, base):
            self.r4p, self.r4m, self.r3p, self.r3m, self.r1p, self.r1m = parts[:6]
            self.stage_p, self.stage_m, self.r2p, self.r2m = parts[6:]
            self.source, self.cut = source, cut

            def send(src, target, index, peer):
                return remote(src, target, sem_z, base + index, z_peer[peer])

            far = source.at[z_at[4]]
            self.all = (
                send(far.at[..., :cut], self.r4p, 0, 2),
                send(far.at[..., cut:], self.r4m, 1, 6),
                send(source.at[z_at[3]], self.r3p, 2, 1),
                send(source.at[z_at[5]], self.r3m, 3, 7),
                send(source.at[z_at[1]], self.r1p, 4, 1),
                send(source.at[z_at[7]], self.r1m, 5, 7),
                send(self.stage_p, self.r2p, 6, 2),
                send(self.stage_m, self.r2m, 7, 6),
            )

        def start(self):
            for copy in self.all[:6]:
                copy.start()

        def middle(self):
            cut = self.cut
            self.all[2].wait_recv()
            self.all[0].wait_recv()
            total = self.source[z_at[2]].astype(F32) + wide(self.r3p)
            self.stage_p[..., cut:] = total[..., cut:].astype(BF16)
            self.stage_p[..., :cut] = (total[..., :cut] + wide(self.r4p)).astype(BF16)
            self.all[6].start()
            self.all[3].wait_recv()
            self.all[1].wait_recv()
            total = self.source[z_at[6]].astype(F32) + wide(self.r3m)
            self.stage_m[..., :cut] = total[..., :cut].astype(BF16)
            self.stage_m[..., cut:] = (total[..., cut:] + wide(self.r4m)).astype(BF16)
            self.all[7].start()

        def finish(self):
            for copy in self.all[4:]:
                copy.wait_recv()
            total = self.source[z_at[0]].astype(F32) + wide(self.r1p) + wide(self.r1m)
            return total + wide(self.r2p) + wide(self.r2m)

    def folds(source, half, y_bufs, z_bufs, cut, y_base, z_base):
        y_fold = YFold(
            lambda at, lanes: source.at[:, at, :, lanes],
            lambda at, lanes: source[:, at, :, lanes],
            cut,
            y_bufs,
            y_base,
        )
        return y_fold, ZFold(half, cut, z_bufs, z_base)

    a_y, a_z = folds(sum_a, half_a, fold_ay, fold_az, CUT_A, 0, 8)
    v_y, v_z = folds(sum_v, half_v, fold_vy, fold_vz, CUT_V, 6, 16)
    b_z = ZFold(sum_b, CUT_B, fold_bz, 0)
    b_y = [
        remote(half_b.at[y_at[k]], recv_by.at[k - 1], sem_y, 11 + k, y_peer[k])
        for k in range(1, NY)
    ]

    own_feats.wait()
    pair_feats.wait_recv()
    for sample in range(SAMPLES):
        pair_cots(sample, 1).wait_recv()

    def spread(value):
        return value.astype(BF16).reshape(NZ, NY, 16, value.shape[1])

    width = D // 2
    for index, which in enumerate((2, 2, 3)):
        value = dot_nn(cot_all[which], feats_half[4 + index])
        sum_b[:, :, :, index * width : (index + 1) * width] = spread(value)
    pl.when(first)(b_z.start)
    for sample in range(SAMPLES):
        pair_cots(sample, 0).wait_recv()
    for index in range(2):
        value = dot_nn(cot_all[0], feats_half[index])
        sum_a[:, :, :, index * width : (index + 1) * width] = spread(value)
    pl.when(first)(a_y.start)
    for index, which in enumerate((0, 1)):
        value = dot_nn(cot_all[which], feats_half[2 + index])
        sum_v[:, :, :, index * width : (index + 1) * width] = spread(value)
    pair_vec.wait_recv()
    vec_sum = vec_acc[0] + vec_acc[1] + vec_sib[0] + vec_sib[1]
    vec_block = jnp.concatenate([vec_sum, jnp.zeros((120, D), F32)], 0).T
    sum_v[:, :, :, 2 * width :] = spread(vec_block)
    pl.when(first)(v_y.start)
    backward_rest(1)
    finish(1)

    @pl.when(jnp.logical_not(first))
    def _():
        b_z.start()
        a_y.start()
        v_y.start()

    def joined(parts):
        return jnp.concatenate(parts, -1)

    def keep(value, start):
        lanes = slice(start, start + value.shape[1])
        fin[0, :, lanes] = value[:8]
        fin[1, :, lanes] = value[8:]

    a_y.middle()
    b_z.middle()
    v_y.middle()
    half_a[...] = joined(a_y.finish()).astype(BF16)
    a_z.start()
    half_v[...] = joined(v_y.finish()).astype(BF16)
    v_z.start()
    half_b[...] = b_z.finish().astype(BF16)
    for copy in b_y:
        copy.start()
    a_z.middle()
    v_z.middle()
    total = half_b[y_at[0]].astype(F32)
    for index, copy in enumerate(b_y):
        copy.wait_recv()
        total = total + recv_by[index].astype(F32)
    keep(total, LANES_A + LANES_V)
    keep(a_z.finish(), 0)
    keep(v_z.finish(), LANES_A)
    swap = remote(fin.at[1 - core], fin_sib, sem_pair, 1, sibling)
    swap.start()
    swap.wait_recv()
    grads_out[core] = fin[core]
    grads_out[1 - core] = fin_sib[...]

    swap.wait_send()
    pair_feats.wait_send()
    pair_vec.wait_send()
    for sample in range(SAMPLES):
        pair_cots(sample, 0).wait_send()
        pair_cots(sample, 1).wait_send()
    for copy in (*a_y.all, *b_z.all, *a_z.all, *v_y.all, *v_z.all, *b_y):
        copy.wait_send()
    for sample in range(SAMPLES):
        for part in range(2):
            for copy in out_halo(sample, part) + back_halo(sample, part):
                copy.wait_send()
        for copy in outputs(sample) + grad_outputs(sample):
            copy.wait()

        @pl.when(jnp.logical_not(last))
        def _():
            edge_relay(sample).wait_send()
            if sample == 0:
                for part in range(2):
                    node_relay(0, part).wait_send()

        @pl.when(jnp.logical_not(first))
        def _():
            edge_return(sample).wait_send()
            for part in range(2):
                node_return(sample, part).wait_send()


def store_kernel(node_out, edge_out, node_grad, edge_grad, grads_hbm, *refs):
    results, held, rows_held, grads, sems = refs[:9], refs[9:13], refs[13:18], refs[18], refs[19]
    grads_load = pltpu.make_async_copy(grads_hbm, grads, sems.at[13])
    grads_load.start()
    sources = (node_out, edge_out, node_grad, edge_grad)
    loads = [
        pltpu.make_async_copy(source, target, sems.at[index])
        for index, (source, target) in enumerate(zip(sources, held))
    ]
    stores = [
        pltpu.make_async_copy(source, target, sems.at[4 + index])
        for index, (source, target) in enumerate(zip(held + rows_held, results))
    ]
    for copy in loads:
        copy.start()
    w1e_rows, w2e_rows, w1n_rows, w2n_rows, vec_rows = rows_held
    grads_load.wait()
    width = D // 2
    places = [(w1e_rows, 0), (w1e_rows, D), (w1e_rows, 2 * D), (w2e_rows, 0)]
    places += [(w1n_rows, 0), (w1n_rows, D), (w2n_rows, 0)]
    for index, (target, start) in enumerate(places):
        lane = index * width if index < 4 else HALF - LANES_B + (index - 4) * width
        for side in range(2):
            target[:, start + side * width : start + (side + 1) * width] = grads[
                side, :, lane : lane + width
            ]
    columns = grads[0, :, 4 * width : 4 * width + 128].T
    vec_rows[...] = columns[:8, :]
    for copy in stores[4:]:
        copy.start()
    for load, copy in zip(loads, stores):
        load.wait()
        copy.start()
    for copy in stores:
        copy.wait()


def local(
    node_in,
    edge_in,
    node_cot,
    edge_cot,
    send_rows,
    sender_row,
    receiver_row,
    edge_count,
    edge_w1,
    edge_w2,
    node_w1,
    node_w2,
    vectors,
):
    anywhere = pl.BlockSpec(memory_space=pl.ANY)
    vmem = pl.BlockSpec(memory_space=pltpu.VMEM)
    smem = pl.BlockSpec(memory_space=pltpu.SMEM)
    both = SAMPLES * ROWS

    def half(*shape):
        return pltpu.VMEM(shape, BF16)

    def full(*shape):
        return pltpu.VMEM(shape, F32)

    def y_parts(lead, lanes, cut):
        low, high = half(*lead, cut), half(*lead, lanes - cut)
        return [low, high, low, high, low, high, low, high]

    def z_parts(lead, lanes, cut):
        return [half(*lead, cut), half(*lead, lanes - cut)] + [half(*lead, lanes)] * 8

    scratch = [
        half(3 * D, D),
        half(D, D),
        half(2 * D, D),
        half(D, D),
        pltpu.VMEM((1, ROWS), jnp.int32),
        pltpu.VMEM((1, ROWS), jnp.int32),
        pltpu.VMEM((1, ROWS), jnp.int32),
        half(8, D),
        full(8, D),
        half(2 * both, D),
        half(7, both, D),
        half(7, 2 * both, D // 2),
        full(both, D),
        full(both, D),
        full(both, 128),
        full(both, D),
        full(both, D),
        full(both, 128),
        half(both, D),
        half(both, D),
        half(both, D),
        half(both, D),
        half(both, D),
        full(both, D),
        full(both, D),
        half(both, D),
        half(both, D),
        half(both, D),
        half(both, D),
        half(both, D),
        half(both, D),
        half(both, D),
        half(4, D, 2 * both),
        full(SAMPLES, 8, D),
        full(SAMPLES, 8, D),
        half(NZ, NY, 16, LANES_A),
        half(NZ, NY, 16, LANES_V),
        half(NZ, NY, 16, LANES_B),
        half(NZ, 16, LANES_A),
        half(NZ, 16, LANES_V),
        half(NY, 16, LANES_B),
        y_parts((NZ, 16), LANES_A, CUT_A),
        y_parts((NZ, 16), LANES_V, CUT_V),
        z_parts((NY, 16), LANES_B, CUT_B),
        z_parts((16,), LANES_A, CUT_A),
        z_parts((16,), LANES_V, CUT_V),
        half(NY - 1, 16, LANES_B),
        full(2, 8, HALF),
        full(8, HALF),
        pltpu.SemaphoreType.DMA((25,)),
        pltpu.SemaphoreType.DMA((2, 12)),
        pltpu.SemaphoreType.DMA((2, 16)),
        pltpu.SemaphoreType.DMA((2, 7)),
        pltpu.SemaphoreType.DMA((2, 15)),
        pltpu.SemaphoreType.DMA((2, 24)),
    ]
    shape = (1, SAMPLES, ROWS, D)
    node_out, edge_out, node_grad, edge_grad, grads = pl.pallas_call(
        kernel,
        out_shape=(
            jax.ShapeDtypeStruct(shape, BF16),
            jax.ShapeDtypeStruct(shape, BF16),
            jax.ShapeDtypeStruct(shape, F32),
            jax.ShapeDtypeStruct(shape, F32),
            jax.ShapeDtypeStruct((2, 8, HALF), F32),
        ),
        in_specs=[anywhere] * 7 + [smem] + [anywhere] * 5,
        out_specs=(anywhere,) * 4 + (vmem,),
        scratch_shapes=scratch,
        compiler_params=pltpu.CompilerParams(
            collective_id=0, has_side_effects=True, vmem_limit_bytes=60 << 20
        ),
        name="layers",
    )(
        node_in,
        edge_in,
        node_cot,
        edge_cot,
        send_rows.reshape(1, ROWS),
        sender_row.reshape(1, ROWS),
        receiver_row.reshape(1, ROWS),
        edge_count,
        edge_w1,
        edge_w2,
        node_w1,
        node_w2,
        vectors,
    )
    rows_of = (3 * D, D, 2 * D, D, 8)
    results = pl.pallas_call(
        store_kernel,
        out_shape=(
            jax.ShapeDtypeStruct(shape, BF16),
            jax.ShapeDtypeStruct(shape, BF16),
            jax.ShapeDtypeStruct(shape, F32),
            jax.ShapeDtypeStruct(shape, F32),
        )
        + tuple(jax.ShapeDtypeStruct((8, rows), F32) for rows in rows_of),
        in_specs=[anywhere] * 5,
        out_specs=(anywhere,) * 9,
        scratch_shapes=[pltpu.VMEM(shape, BF16)] * 2
        + [pltpu.VMEM(shape, F32)] * 2
        + [pltpu.VMEM((8, rows), F32) for rows in rows_of]
        + [pltpu.VMEM((2, 8, HALF), F32), pltpu.SemaphoreType.DMA((14,))],
        name="store",
    )(node_out, edge_out, node_grad, edge_grad, grads)
    return results[:4] + tuple(value.T[None] for value in results[4:8]) + (results[8][None],)


def solution(mesh):
    in_specs = (
        P("dp", "dom", None),
        P("dp", "dom", None),
        P("dp", "dom", None),
        P("dp", "dom", None),
        P("dom"),
        P("dom"),
        P("dom"),
        P("dom"),
        P("segment", None, None),
        P("segment", None, None),
        P("segment", None, None),
        P("segment", None, None),
        P("segment", None, None),
    )
    out_specs = (
        P("segment", "dp", "dom", None),
        P("segment", "dp", "dom", None),
        P("segment", "dp", "dom", None),
        P("segment", "dp", "dom", None),
        P("segment", None, ("dom", "dp")),
        P("segment", None, ("dom", "dp")),
        P("segment", None, ("dom", "dp")),
        P("segment", None, ("dom", "dp")),
        P("segment", None, ("dom", "dp")),
    )
    return jax.shard_map(local, mesh=mesh, in_specs=in_specs, out_specs=out_specs, check_vma=False)
```
